256 devices in a mesh: patch: 8 (over z), expert: 16 (over y, x), hidden: 2 (over core).
Axes of the slice: x: 4, y: 4, z: 8, core: 2. Of those that a mesh axis runs over, the one named last changes fastest.
Arguments:
- tokens: bfloat16 [16384, 4096], P(('patch', 'expert')), may hold values from -6 to 6
- cotangent: bfloat16 [16384, 4096], P(('patch', 'expert')), may hold values from -1.5 to 1.5
- w_in: bfloat16 [16, 4096, 4096], P('expert', None, ('patch', 'hidden')), may hold values from -0.09375 to 0.09375
- w_out: bfloat16 [16, 4096, 4096], P('expert', ('patch', 'hidden')), may hold values from -0.09375 to 0.09375
- gates: float32 [16, 1024], P('expert'), may hold values from 0.1 to 1
- picks: int32 [16, 1024], replicated, may hold values from 0 to 16383, as said below
- counts: int32 [16], replicated, may hold values from 512 to 1024, as said below
Outputs:
- d_tokens: bfloat16 [16384, 4096], P(('patch', 'expert'), 'hidden')
- d_w_in: bfloat16 [16, 4096, 4096], P('expert', None, ('patch', 'hidden'))
- d_w_out: bfloat16 [16, 4096, 4096], P('expert', ('patch', 'hidden'))
- d_gates: float32 [16, 1024], P('expert', ('patch', 'hidden'))
The draws below stay inside these ranges and needn't reach their ends.
Inputs may be any that keep to these rules, and one draw needn't show every extreme that they name: `picks`: each expert's list names distinct rows. Slots from counts[e] on are padding and name rows that are ignored. Within one expert's aligned block of 128 slots, at most 2 slots name rows of one aligned block of 128 rows, and this bound is reached in every draw. `counts`: some expert has all 1024 slots live.
All inputs are finite; a program needn't handle non-finite values.
Results may differ from the reference program's by a relative error of at most 0.023.
Values may be sent and summed in bfloat16 or wider, within the bound.
A program may use at most 128 MiB of HBM per device.

```python
import jax
import jax.numpy as jnp
from jax import lax

D = 4096
FF = 4096
TOK_DEV = 128
EXPERTS = 16
TOKENS = 16384
CAP = 1024
SOURCES = 128
SLOTS = 128
N_PATCH = 8
N_HIDDEN = 2


def draw_counts(key, part):
    key = jax.random.fold_in(key, 7)
    first_key, second_key = jax.random.split(key)
    fullest = jax.random.randint(first_key, (), 0, EXPERTS)
    drawn = jax.random.randint(second_key, (EXPERTS,), CAP // 2, CAP + 1)
    return jnp.where(jnp.arange(EXPERTS) == fullest, CAP, drawn).astype(jnp.int32)


def draw_picks(key, part):
    key = jax.random.fold_in(key, 11)
    first_key, second_key, third_key = jax.random.split(key, 3)
    blocks = CAP // SLOTS
    width_used = min(SLOTS, SOURCES)
    group_count = SLOTS // width_used
    scores = jax.random.randint(first_key, (EXPERTS, blocks, 1, SOURCES), 0, 65536) * SOURCES + jnp.arange(SOURCES, dtype=jnp.int32)
    order = jnp.argsort(scores, axis=-1)[..., :width_used].astype(jnp.int32)
    choose = jax.random.randint(second_key, (EXPERTS, blocks, group_count, width_used), 0, 2)
    choose = choose.at[..., 0].set(1).at[..., 1].set(0)
    earlier = jnp.roll(order, 1, axis=-1)
    source = jnp.where(choose == 1, order, earlier)
    repeat = 1 - choose
    slot_code = (jnp.arange(blocks, dtype=jnp.int32)[:, None, None] * group_count + jnp.arange(group_count, dtype=jnp.int32)[:, None]) * 2 + repeat
    row_scores = jax.random.randint(third_key, (EXPERTS, SOURCES, TOK_DEV), 0, 65536) * TOK_DEV + jnp.arange(TOK_DEV, dtype=jnp.int32)
    row_order = jnp.argsort(row_scores, axis=-1).astype(jnp.int32)
    expert_ids = jnp.arange(EXPERTS, dtype=jnp.int32)[:, None, None, None]
    local_row = row_order[expert_ids, source, slot_code]
    return (source * TOK_DEV + local_row).reshape(EXPERTS, CAP).astype(jnp.int32)


def steps_of(stream_key, dims, shards, smallest, largest):
    def one(dim, shards_of):
        heights = jax.random.uniform(jax.random.fold_in(jax.random.fold_in(stream_key, 6), dim), (shards_of,), jnp.float32, smallest / len(shards), largest / len(shards))
        return jnp.repeat(jnp.exp(heights), dims[dim] // shards_of).reshape((-1,) + (1,) * (len(dims) - dim - 1))

    gain = one(*shards[0])
    for cut in shards[1:]:
        gain = gain * one(*cut)
    return gain


def scatter_about(key, extent, scale, most, pieces=(), held_as=jnp.bfloat16):
    level = steps_of(key, extent, pieces, -0.22, 0.18) if pieces else 1.0
    result = jax.random.normal(key, extent, jnp.float32) * scale * level
    return jnp.minimum(jnp.maximum(result, -most), most).astype(held_as)


def setup_inputs(seed: int = 0) -> dict:
    splits = jax.random.split(jax.random.key(seed), 8)
    tokens = scatter_about(splits[0], (TOKENS, D), 1.0, 6.0, ((0, 128),))
    cotangent = scatter_about(splits[1], (TOKENS, D), 0.25, 1.5, ((0, 128),))
    w_in = scatter_about(splits[2], (EXPERTS, D, FF), D ** -0.5, 0.09375, ((0, 16), (2, 16)))
    w_out = scatter_about(splits[3], (EXPERTS, FF, D), FF ** -0.5, 0.09375, ((0, 16), (1, 16)))
    gates = jnp.clip(0.1 + 0.9 * jax.random.uniform(splits[4], (EXPERTS, CAP), jnp.float32) ** steps_of(splits[4], (EXPERTS, CAP), ((0, 16),), -0.2, 0.2), 0.1, 1.0)
    picks = draw_picks(jax.random.fold_in(splits[7], 71), 0)
    counts = draw_counts(jax.random.fold_in(splits[7], 71), 0)
    return {"tokens": tokens, "cotangent": cotangent, "w_in": w_in, "w_out": w_out, "gates": gates, "picks": picks, "counts": counts}


inv_root_two = 0.7071067811865476
inv_root_two_pi = 0.3989422804014327


def gelu_parts(pre):
    normal_cdf = 0.5 * (1.0 + lax.erf(pre * inv_root_two))
    density = jnp.exp(-0.5 * pre * pre) * inv_root_two_pi
    return pre * normal_cdf, normal_cdf + pre * density


def reference(tokens, cotangent, w_in, w_out, gates, picks, counts):
    live = jnp.arange(CAP, dtype=jnp.int32)[None, :] < counts[:, None]
    groups = N_PATCH * N_HIDDEN
    group_width = FF // groups

    def one_expert(inputs):
        pick_row, live_row, gate_row, weight_in, weight_out = inputs
        picked = jnp.where(live_row[:, None], jnp.take(tokens, pick_row, axis=0), jnp.zeros((), jnp.bfloat16)).astype(jnp.bfloat16)
        grad_rows = jnp.where(live_row[:, None], jnp.take(cotangent, pick_row, axis=0), jnp.zeros((), jnp.bfloat16)).astype(jnp.bfloat16)
        pre = jnp.dot(picked, weight_in, preferred_element_type=jnp.float32)
        act, slope = gelu_parts(pre)
        act_b = act.astype(jnp.bfloat16)
        back_act = lax.dot_general(grad_rows, weight_out, (((1,), (1,)), ((), ())), preferred_element_type=jnp.float32)
        gate_col = gate_row[:, None]
        gate_grad = jnp.sum(act * back_act, axis=1)
        back_pre = (gate_col * back_act * slope).astype(jnp.bfloat16)
        gated_rows = (gate_col * grad_rows.astype(jnp.float32)).astype(jnp.bfloat16)
        grad_in = lax.dot_general(picked, back_pre, (((0,), (0,)), ((), ())), preferred_element_type=jnp.float32).astype(jnp.bfloat16)
        grad_out = lax.dot_general(act_b, gated_rows, (((0,), (0,)), ((), ())), preferred_element_type=jnp.float32).astype(jnp.bfloat16)

        def add_group(total, group):
            begin = (group * group_width).astype(jnp.int32)
            piece_grad = lax.dynamic_slice_in_dim(back_pre, begin, group_width, 1)
            piece_weight = lax.dynamic_slice_in_dim(weight_in, begin, group_width, 1)
            term = lax.dot_general(piece_grad, piece_weight, (((1,), (1,)), ((), ())), preferred_element_type=jnp.float32)
            rounded = lax.optimization_barrier(term.astype(jnp.bfloat16))
            return total + rounded.astype(jnp.float32), None

        total, _ = lax.scan(add_group, jnp.zeros((CAP, D), jnp.float32), jnp.arange(groups, dtype=jnp.int32))
        slot_grad = total.astype(jnp.bfloat16)
        return gate_grad, grad_in, grad_out, slot_grad

    d_gates, d_w_in, d_w_out, slot_grads = lax.map(one_expert, (picks, live, gates, w_in, w_out))
    masked = jnp.where(live[:, :, None], slot_grads.astype(jnp.float32), jnp.zeros((), jnp.float32))
    summed = jnp.zeros((TOKENS, D), jnp.float32).at[picks.reshape(-1)].add(masked.reshape(-1, D))
    return summed.astype(jnp.bfloat16), d_w_in, d_w_out, d_gates
```

```python
import functools

import jax
import jax.numpy as jnp
from jax import lax
from jax.experimental import pallas as pl
from jax.experimental.pallas import tpu as pltpu
from jax.sharding import PartitionSpec as P

inv_root_two = 0.7071067811865476
inv_root_two_pi = 0.3989422804014327


def gelu_parts(pre):
    normal_cdf = 0.5 * (1.0 + lax.erf(pre * inv_root_two))
    density = jnp.exp(-0.5 * pre * pre) * inv_root_two_pi
    return (pre * normal_cdf, normal_cdf + pre * density)


def general(tokens, cotangent, w_in, w_out, gates, picks, counts):
    tok_dev, width = tokens.shape
    patch_count = lax.axis_size("patch")
    expert_count = lax.axis_size("expert")
    hidden_parts = lax.axis_size("hidden")
    capacity = picks.shape[1]
    slots = capacity // patch_count
    sources = patch_count * expert_count
    bound = 2 * max(1, slots // sources)
    limit = sources * bound
    patch_here = lax.axis_index("patch")
    expert_here = lax.axis_index("expert")
    source_here = patch_here * expert_count + expert_here
    slot_ids = jnp.arange(capacity, dtype=jnp.int32)
    live = slot_ids[None, :] < counts[:, None]
    holder = picks // tok_dev
    local_row = picks % tok_dev
    mine = (
        ((holder == source_here) & live).reshape(expert_count, patch_count, slots).astype(jnp.int32)
    )
    order_mine = jnp.cumsum(mine, axis=2) - 1
    expert_ids = jnp.arange(expert_count, dtype=jnp.int32)[:, None, None]
    patch_ids = jnp.arange(patch_count, dtype=jnp.int32)[None, :, None]
    position = (patch_ids * expert_count + expert_ids) * bound + order_mine
    position = jnp.where(mine == 1, position, limit)
    send_table = (
        jnp.full((limit,), tok_dev, jnp.int32)
        .at[position.reshape(-1)]
        .set(local_row.reshape(-1), mode="drop")
    )
    send_rows = jnp.take(tokens, send_table, axis=0, mode="fill", fill_value=0).reshape(
        sources, bound, width
    )
    send_grads = jnp.take(cotangent, send_table, axis=0, mode="fill", fill_value=0).reshape(
        sources, bound, width
    )
    came_rows, came_grads = (
        lax.all_to_all(send_rows, ("patch", "expert"), split_axis=0, concat_axis=0, tiled=True),
        lax.all_to_all(send_grads, ("patch", "expert"), split_axis=0, concat_axis=0, tiled=True),
    )
    my_picks = lax.dynamic_slice_in_dim(picks, expert_here, 1, 0)[0]
    block_picks = lax.dynamic_slice_in_dim(my_picks, patch_here * slots, slots, 0)
    count_here = lax.dynamic_slice_in_dim(counts, expert_here, 1, 0)[0]
    within = jnp.arange(slots, dtype=jnp.int32)
    block_live = patch_here * slots + within < count_here
    block_holder = block_picks // tok_dev
    earlier_same = (
        (block_holder[:, None] == block_holder[None, :])
        & block_live[None, :]
        & (within[None, :] < within[:, None])
    )
    block_order = jnp.sum(earlier_same.astype(jnp.int32), axis=1)
    came_index = jnp.where(block_live, block_holder * bound + block_order, limit)
    block_rows = jnp.take(
        came_rows.reshape(limit, width), came_index, axis=0, mode="fill", fill_value=0
    )
    block_grads = jnp.take(
        came_grads.reshape(limit, width), came_index, axis=0, mode="fill", fill_value=0
    )
    slot_rows, grad_rows = (
        lax.all_gather(block_rows, "patch", axis=0, tiled=True),
        lax.all_gather(block_grads, "patch", axis=0, tiled=True),
    )
    gate_col = gates[0][:, None]
    weight_in = w_in[0]
    weight_out = w_out[0]
    unit_count = weight_in.shape[1]
    pre = jnp.dot(slot_rows, weight_in, preferred_element_type=jnp.float32)
    act, slope = gelu_parts(pre)
    act_b = act.astype(jnp.bfloat16)
    back_act = lax.dot_general(
        grad_rows, weight_out, (((1,), (1,)), ((), ())), preferred_element_type=jnp.float32
    )
    gate_grad = jnp.sum(act * back_act, axis=1)
    back_pre = (gate_col * back_act * slope).astype(jnp.bfloat16)
    gated_rows = (gate_col * grad_rows.astype(jnp.float32)).astype(jnp.bfloat16)
    grad_in = lax.dot_general(
        slot_rows, back_pre, (((0,), (0,)), ((), ())), preferred_element_type=jnp.float32
    )
    grad_out = lax.dot_general(
        act_b, gated_rows, (((0,), (0,)), ((), ())), preferred_element_type=jnp.float32
    )
    gate_terms = gate_grad.reshape(patch_count * hidden_parts, slots // hidden_parts)
    d_gates = lax.psum_scatter(gate_terms, ("patch", "hidden"), scatter_dimension=0, tiled=True)
    selector = (jnp.arange(tok_dev, dtype=jnp.int32)[:, None] == send_table[None, :]).astype(
        jnp.bfloat16
    )
    back_blocks = back_pre.reshape(patch_count, slots, unit_count)
    weight_halves = weight_in.reshape(hidden_parts, width // hidden_parts, unit_count)
    slot_terms = jnp.einsum(
        "psf,hdf->phsd", back_blocks, weight_halves, preferred_element_type=jnp.float32
    ).astype(jnp.bfloat16)
    slot_terms = slot_terms.reshape(patch_count * hidden_parts, slots, width // hidden_parts)
    slot_sum = lax.psum_scatter(
        slot_terms, ("patch", "hidden"), scatter_dimension=0, tiled=True
    ).astype(jnp.float32)[0]
    slot_grad = slot_sum.astype(jnp.bfloat16)
    going_back = (
        jnp.zeros((limit, width // hidden_parts), jnp.bfloat16)
        .at[came_index]
        .set(slot_grad, mode="drop")
    )
    send_width = width // hidden_parts
    returned = lax.all_to_all(
        going_back.reshape(sources, bound, send_width),
        ("patch", "expert"),
        split_axis=0,
        concat_axis=0,
        tiled=True,
    )
    returned = returned.reshape(limit, send_width)
    token_grad = jnp.dot(selector, returned, preferred_element_type=jnp.float32)
    d_tokens = token_grad.astype(jnp.bfloat16)
    return (
        d_tokens,
        grad_in.astype(jnp.bfloat16)[None],
        grad_out.astype(jnp.bfloat16)[None],
        d_gates,
    )


MESH = pl.DeviceIdType.MESH
f32 = jnp.float32
bf16 = jnp.bfloat16
ROWS_PER_PAIR = 16
PIECES = 4


def contract(a, b, dim_a, dim_b):
    return lax.dot_general(a, b, (((dim_a,), (dim_b,)), ((), ())), preferred_element_type=f32)


def row_sums(x):
    ones = jnp.ones((8, x.shape[1]), bf16)
    high = x.astype(bf16)
    low = (x - high.astype(f32)).astype(bf16)
    return (contract(ones, high, 1, 1) + contract(ones, low, 1, 1))[0:1]


def kernel(
    planes,
    experts,
    cap,
    tokens,
    cotangent,
    w_in_hbm,
    w_out_hbm,
    pick_sel,
    pack_sel,
    gate_ref,
    d_tok_hbm,
    d_in_hbm,
    d_out_hbm,
    gate_total,
    held,
    going,
    came,
    allrows,
    win,
    wout,
    act_s,
    back_s,
    home,
    part_out,
    part_in,
    sum_out,
    sum_in,
    grad_go,
    grad_came,
    d_tok,
    d_in,
    d_out,
    gate_lo,
    gate_hi,
    gate_all,
    load_sem,
    go_send,
    go_recv,
    ring_send,
    ring_recv,
    twin_send,
    twin_recv,
    part_send,
    part_recv,
    sum_send,
    sum_recv,
    grad_send,
    grad_recv,
    gate_send,
    gate_recv,
    store_sem,
):
    z = lax.axis_index("patch")
    e = lax.axis_index("expert")
    c = lax.axis_index("hidden")
    other = 1 - c
    up = (lax.rem(z + 1, planes), e, c)
    down = (lax.rem(z + planes - 1, planes), e, c)
    twin = (z, e, other)
    width = PIECES * held.shape[3]
    piece = held.shape[3]
    half = cap // 2
    plane_peers = [(z, lax.rem(e + k, experts), c) for k in range(1, experts)]
    me = z * 2 + c
    column_ids = [lax.rem(me + k, 2 * planes) for k in range(1, 2 * planes)]
    column_peers = [(i // 2, e, lax.rem(i, 2)) for i in column_ids]

    barrier = pltpu.get_barrier_semaphore()
    for peer in plane_peers + column_peers:
        pl.semaphore_signal(barrier, inc=1, device_id=peer, device_id_type=MESH)

    loads = []
    for a, ref in enumerate((tokens, cotangent)):
        for j in range(2):
            col = pl.multiple_of((2 * c + j) * piece, piece)
            cp = pltpu.make_async_copy(
                ref.at[:, pl.ds(col, piece)], held.at[a, j], load_sem.at[2 * a + j]
            )
            cp.start()
            loads.append(cp)
    load_in = pltpu.make_async_copy(w_in_hbm, win, load_sem.at[4])
    load_out = pltpu.make_async_copy(w_out_hbm, wout, load_sem.at[5])
    load_in.start()
    load_out.start()

    pl.semaphore_wait(barrier, len(plane_peers) + len(column_peers))

    def remote(src, dst, s, r, dev):
        return pltpu.make_async_remote_copy(
            src_ref=src, dst_ref=dst, send_sem=s, recv_sem=r, device_id=dev, device_id_type=MESH
        )

    def plane_copy(src, dst, ssem, rsem, k):
        to = pl.multiple_of(lax.rem(e + k, experts) * ROWS_PER_PAIR, ROWS_PER_PAIR)
        at = pl.multiple_of(e * ROWS_PER_PAIR, ROWS_PER_PAIR)
        return remote(
            src.at[pl.ds(to, ROWS_PER_PAIR)],
            dst.at[pl.ds(at, ROWS_PER_PAIR)],
            ssem.at[k],
            rsem.at[k],
            plane_peers[k - 1],
        )

    own_rows = pl.ds(pl.multiple_of(e * ROWS_PER_PAIR, ROWS_PER_PAIR), ROWS_PER_PAIR)

    for a in range(2):
        for j in range(2):
            loads[2 * a + j].wait()
            going[a, j] = contract(pick_sel[...], held[a, j], 1, 0).astype(bf16)
            came[a, j, own_rows, :] = going[a, j, own_rows, :]
            for k in range(1, experts):
                plane_copy(
                    going.at[a, j], came.at[a, j], go_send.at[a, j], go_recv.at[a, j], k
                ).start()

    def ring_up(a, j, t):
        q = 2 * c + j
        return remote(
            allrows.at[a, q, t, pl.ds(0, half)],
            allrows.at[a, q, t + 1, pl.ds(0, half)],
            ring_send.at[0, a, j, t],
            ring_recv.at[0, a, j, t + 1],
            up,
        )

    def ring_down(a, j, t):
        q = 2 * c + j
        return remote(
            allrows.at[a, q, t, pl.ds(half, half)],
            allrows.at[a, q, t + 1, pl.ds(half, half)],
            ring_send.at[1, a, j, t],
            ring_recv.at[1, a, j, t + 1],
            down,
        )

    def twin_copy(a, j, t):
        q = 2 * c + j
        return remote(
            allrows.at[a, q, t],
            allrows.at[a, q, t],
            twin_send.at[a, j, t],
            twin_recv.at[a, j, t],
            twin,
        )

    def part_copy(j, t):
        slot = lax.rem(t, 2)
        return remote(
            part_out.at[slot, j], part_in.at[t, j], part_send.at[t, j], part_recv.at[t, j], twin
        )

    def sum_up(j, t):
        return remote(
            sum_out.at[lax.rem(t, 2), j, pl.ds(0, half)],
            sum_in.at[t, j, pl.ds(0, half)],
            sum_send.at[0, j, t],
            sum_recv.at[0, j, t],
            up,
        )

    def sum_down(j, t):
        return remote(
            sum_out.at[lax.rem(t, 2), j, pl.ds(half, half)],
            sum_in.at[t, j, pl.ds(half, half)],
            sum_send.at[1, j, t],
            sum_recv.at[1, j, t],
            down,
        )

    for a in range(2):
        for j in range(2):
            for k in range(1, experts):
                plane_copy(
                    going.at[a, j], came.at[a, j], go_send.at[a, j], go_recv.at[a, j], k
                ).wait()
            allrows[a, 2 * c + j, 0] = contract(pack_sel[...], came[a, j], 1, 0).astype(bf16)
            ring_up(a, j, 0).start()
            ring_down(a, j, 0).start()
            twin_copy(a, j, 0).start()
    load_in.wait()
    load_out.wait()

    def step(t, carry):
        for a in range(2):
            for j in range(2):

                @pl.when(t > 0)
                def _():
                    ring_up(a, j, t - 1).wait_recv()

                    @pl.when(t < planes - 1)
                    def _():
                        ring_up(a, j, t).start()

                    ring_down(a, j, t - 1).wait_recv()

                    @pl.when(t < planes - 1)
                    def _():
                        ring_down(a, j, t).start()

                    twin_copy(a, j, t).start()

        for a in range(2):
            for j in range(2):
                twin_copy(a, j, t).wait_recv()
        pre = contract(allrows[0, 0, t], win[0], 1, 0)
        back = contract(allrows[1, 0, t], wout[:, 0:piece], 1, 1)
        for q in range(1, PIECES):
            pre += contract(allrows[0, q, t], win[q], 1, 0)
            back += contract(allrows[1, q, t], wout[:, q * piece : (q + 1) * piece], 1, 1)
        act, slope = gelu_parts(pre)
        gate = gate_ref[t]
        act_s[t] = (gate * act).astype(bf16)
        back_pre = (gate * back * slope).astype(bf16)
        back_s[t] = back_pre
        gate_row = row_sums(act * back)
        gate_lo[pl.ds(lax.rem(z + planes - t, planes), 1), 0:cap] = gate_row
        gate_hi[pl.ds(lax.rem(z + t, planes), 1), 0:cap] = gate_row

        for j in range(2):

            @pl.when(t > 1)
            def _():
                part_copy(j, t - 2).wait_send()

            part_out[lax.rem(t, 2), j] = contract(back_pre, win[2 * other + j], 1, 1).astype(bf16)
            part_copy(j, t).start()
        for j in range(2):
            own = contract(back_pre, win[2 * c + j], 1, 1)
            part_copy(j, t).wait_recv()
            own += part_in[t, j].astype(f32)

            @pl.when(t == 0)
            def _():
                home[j] = own

            @pl.when(t > 2)
            def _():
                sum_up(j, t - 2).wait_send()
                sum_down(j, t - 2).wait_send()

            @pl.when(t > 1)
            def _():
                sum_up(j, t - 1).wait_recv()
                sum_down(j, t - 1).wait_recv()
                sum_out[lax.rem(t, 2), j] = (own + sum_in[t - 1, j].astype(f32)).astype(bf16)

            @pl.when(t == 1)
            def _():
                sum_out[lax.rem(t, 2), j] = own.astype(bf16)

            @pl.when(t > 0)
            def _():
                sum_up(j, t).start()
                sum_down(j, t).start()

        return carry

    lax.fori_loop(0, planes, step, 0)

    lane = lax.broadcasted_iota(jnp.int32, gate_lo.shape, 1)
    gate_all[me] = jnp.where(
        lane < half, gate_lo[...], jnp.where(lane < cap, gate_hi[...], 0.0)
    )

    def gate_copy(k):
        return remote(
            gate_all.at[me], gate_all.at[me], gate_send.at[k], gate_recv.at[k], column_peers[k - 1]
        )

    for k in range(1, 2 * planes):
        gate_copy(k).start()

    rows = planes * cap
    act_all = act_s[...].reshape(rows, act_s.shape[2])
    for q in range(PIECES):
        d_out[q] = contract(act_all, allrows[1, q].reshape(rows, piece), 0, 0).astype(bf16)

    last = planes - 1
    for j in range(2):
        sum_up(j, last).wait_recv()
        sum_down(j, last).wait_recv()
        slot_grad = (home[j] + sum_in[last, j].astype(f32)).astype(bf16)
        grad_go[j] = contract(pack_sel[...], slot_grad, 0, 0).astype(bf16)
        grad_came[j, own_rows, :] = grad_go[j, own_rows, :]
        for k in range(1, experts):
            plane_copy(grad_go.at[j], grad_came.at[j], grad_send.at[j], grad_recv.at[j], k).start()

    stores = []
    for q in range(PIECES):
        cp = pltpu.make_async_copy(
            d_out.at[q], d_out_hbm.at[:, pl.ds(q * piece, piece)], store_sem.at[q]
        )
        cp.start()
        stores.append(cp)
    back_all = back_s[...].reshape(rows, back_s.shape[2])
    for q in range(PIECES):
        turned = contract(back_all, allrows[0, q].reshape(rows, piece), 0, 0)
        d_in[q] = turned.T.astype(bf16)
        cp = pltpu.make_async_copy(d_in.at[q], d_in_hbm.at[q], store_sem.at[PIECES + q])
        cp.start()
        stores.append(cp)

    for j in range(2):
        for k in range(1, experts):
            plane_copy(grad_go.at[j], grad_came.at[j], grad_send.at[j], grad_recv.at[j], k).wait()
        d_tok[j] = contract(pick_sel[...], grad_came[j], 0, 0).astype(bf16)
        cp = pltpu.make_async_copy(
            d_tok.at[j], d_tok_hbm.at[:, pl.ds(j * piece, piece)], store_sem.at[2 * PIECES + j]
        )
        cp.start()
        stores.append(cp)

    for k in range(1, 2 * planes):
        gate_copy(k).wait()
    total = gate_all[0]
    for i in range(1, 2 * planes):
        total += gate_all[i]
    gate_total[...] = total

    for a in range(2):
        for j in range(2):
            for t in range(planes):
                twin_copy(a, j, t).wait_send()
                if t < planes - 1:
                    ring_up(a, j, t).wait_send()
                    ring_down(a, j, t).wait_send()
    for j in range(2):
        for t in (planes - 2, planes - 1):
            part_copy(j, t).wait_send()
            sum_up(j, t).wait_send()
            sum_down(j, t).wait_send()
    for cp in stores:
        cp.wait()


def fast(cap, tokens, cotangent, w_in, w_out, pick_sel, pack_sel, gate_steps):
    planes = lax.axis_size("patch")
    experts = lax.axis_size("expert")
    tok_dev, width = tokens.shape
    units = w_in.shape[1]
    piece = width // PIECES
    pairs = experts * ROWS_PER_PAIR
    vmem = pl.BlockSpec(memory_space=pltpu.VMEM)
    hbm = pl.BlockSpec(memory_space=pl.ANY)
    dma = pltpu.SemaphoreType.DMA
    scratch = [
        pltpu.VMEM((2, 2, tok_dev, piece), bf16),
        pltpu.VMEM((2, 2, pairs, piece), bf16),
        pltpu.VMEM((2, 2, pairs, piece), bf16),
        pltpu.VMEM((2, PIECES, planes, cap, piece), bf16),
        pltpu.VMEM((PIECES, piece, units), bf16),
        pltpu.VMEM((units, width), bf16),
        pltpu.VMEM((planes, cap, units), bf16),
        pltpu.VMEM((planes, cap, units), bf16),
        pltpu.VMEM((2, cap, piece), f32),
        pltpu.VMEM((2, 2, cap, piece), bf16),
        pltpu.VMEM((planes, 2, cap, piece), bf16),
        pltpu.VMEM((2, 2, cap, piece), bf16),
        pltpu.VMEM((planes, 2, cap, piece), bf16),
        pltpu.VMEM((2, pairs, piece), bf16),
        pltpu.VMEM((2, pairs, piece), bf16),
        pltpu.VMEM((2, tok_dev, piece), bf16),
        pltpu.VMEM((PIECES, piece, units), bf16),
        pltpu.VMEM((PIECES, units, piece), bf16),
        pltpu.VMEM((planes, 256), f32),
        pltpu.VMEM((planes, 256), f32),
        pltpu.VMEM((2 * planes, planes, 256), f32),
        dma((6,)),
        dma((2, 2, experts)),
        dma((2, 2, experts)),
        dma((2, 2, 2, planes)),
        dma((2, 2, 2, planes)),
        dma((2, 2, planes)),
        dma((2, 2, planes)),
        dma((planes, 2)),
        dma((planes, 2)),
        dma((2, 2, planes)),
        dma((2, 2, planes)),
        dma((2, experts)),
        dma((2, experts)),
        dma((2 * planes,)),
        dma((2 * planes,)),
        dma((2 * PIECES + 2,)),
    ]
    return pl.pallas_call(
        functools.partial(kernel, planes, experts, cap),
        out_shape=(
            jax.ShapeDtypeStruct((tok_dev, width // 2), bf16),
            jax.ShapeDtypeStruct((PIECES, piece, units), bf16),
            jax.ShapeDtypeStruct((units, width), bf16),
            jax.ShapeDtypeStruct((planes, 256), f32),
        ),
        in_specs=[hbm, hbm, hbm, hbm, vmem, vmem, vmem],
        out_specs=(hbm, hbm, hbm, vmem),
        scratch_shapes=scratch,
        compiler_params=pltpu.CompilerParams(
            collective_id=0, has_side_effects=True, vmem_limit_bytes=60 * 2**20
        ),
    )(
        tokens,
        cotangent,
        w_in.reshape(PIECES, piece, units),
        w_out,
        pick_sel,
        pack_sel,
        gate_steps,
    )


def local(tokens, cotangent, w_in, w_out, gates, picks, counts):
    tok_dev, width = tokens.shape
    planes = lax.axis_size("patch")
    experts = lax.axis_size("expert")
    hidden_parts = lax.axis_size("hidden")
    capacity = picks.shape[1]
    sources = planes * experts
    slots = capacity // planes
    cap = 5 * slots // 4
    half = cap // 2
    z = lax.axis_index("patch")
    e = lax.axis_index("expert")
    c = lax.axis_index("hidden")
    place = jnp.arange(capacity, dtype=jnp.int32)
    codes = jnp.where(place[None, :] < counts[:, None], picks, -1)
    plane_rows = tok_dev * experts
    plane_ids = jnp.arange(planes, dtype=jnp.int32)
    loads = jnp.sum(
        (
            (codes[:, :, None] >= plane_ids * plane_rows)
            & (codes[:, :, None] < (plane_ids + 1) * plane_rows)
        ).astype(jnp.int32),
        axis=1,
    )
    fits = jnp.max(loads) <= cap

    tok_ids = jnp.arange(tok_dev, dtype=jnp.int32)
    source = z * experts + e
    before = (tok_ids[:, None] < tok_ids[None, :]).astype(bf16)
    taken = jnp.any(codes[:, :, None] == source * tok_dev + tok_ids, axis=1)
    order = jnp.dot(taken.astype(bf16), before, preferred_element_type=f32).astype(jnp.int32)
    pair_ids = jnp.arange(ROWS_PER_PAIR, dtype=jnp.int32)
    pick_sel = (
        (taken[:, None, :] & (order[:, None, :] == pair_ids[None, :, None]))
        .astype(bf16)
        .reshape(experts * ROWS_PER_PAIR, tok_dev)
    )

    mine = lax.dynamic_slice_in_dim(codes, e, 1, 0)[0]
    holder = jnp.where(mine < 0, -1, mine // tok_dev)
    row = mine % tok_dev
    source_ids = jnp.arange(sources, dtype=jnp.int32)
    by_holder = (holder[:, None] == source_ids).astype(bf16)
    by_row = (row[:, None] == tok_ids).astype(bf16)
    chosen = contract(by_holder, by_row, 0, 0)
    ranks = jnp.dot(chosen.astype(bf16), before, preferred_element_type=f32)
    sizes = jnp.sum(chosen, axis=1)
    ahead = (source_ids[:, None] // experts == source_ids[None, :] // experts) & (
        source_ids[None, :] < source_ids[:, None]
    )
    offsets = jnp.sum(jnp.where(ahead, sizes[None, :], 0.0), axis=1)
    dest = (offsets[:, None] + ranks).astype(bf16)
    spot = jnp.sum(
        jnp.dot(by_holder, dest, preferred_element_type=f32) * by_row.astype(f32), axis=1
    ).astype(jnp.int32)
    block = holder // experts
    my_sizes = lax.dynamic_slice_in_dim(sizes, z * experts, experts, 0).astype(jnp.int32)
    my_offsets = lax.dynamic_slice_in_dim(offsets, z * experts, experts, 0).astype(jnp.int32)
    target = jnp.where(
        pair_ids[None, :] < my_sizes[:, None], my_offsets[:, None] + pair_ids[None, :], -1
    ).reshape(-1)
    pack_sel = (jnp.arange(cap, dtype=jnp.int32)[:, None] == target[None, :]).astype(bf16)
    when = jnp.where(spot < half, (z - block + planes) % planes, (block - z + planes) % planes)
    step_spot = jnp.where(mine < 0, -1, when * cap + spot)
    gate_steps = jnp.sum(
        jnp.where(
            jnp.arange(planes * cap, dtype=jnp.int32)[:, None] == step_spot[None, :],
            gates[0][None, :],
            0.0,
        ),
        axis=1,
    ).reshape(planes, cap, 1)
    table_spot = jnp.where(mine < 0, -1, block * 256 + spot)
    per_device = slots // hidden_parts
    my_spot = lax.dynamic_slice_in_dim(
        table_spot, (z * hidden_parts + c) * per_device, per_device, 0
    )

    def quick(tokens, cotangent, w_in, w_out, gates, picks, counts):
        d_tokens, d_in, d_out, total = fast(
            cap, tokens, cotangent, w_in[0], w_out[0], pick_sel, pack_sel, gate_steps
        )
        flat = total.reshape(-1)
        found = my_spot[:, None] == jnp.arange(flat.shape[0], dtype=jnp.int32)[None, :]
        d_gates = jnp.sum(jnp.where(found, flat[None, :], 0.0), axis=1)
        return (d_tokens, d_in.reshape(w_in.shape), d_out[None], d_gates[None])

    return lax.cond(fits, quick, general, tokens, cotangent, w_in, w_out, gates, picks, counts)


def solution(mesh):
    in_specs = (
        P(("patch", "expert"), None),
        P(("patch", "expert"), None),
        P("expert", None, ("patch", "hidden")),
        P("expert", ("patch", "hidden"), None),
        P("expert", None),
        P(),
        P(),
    )
    out_specs = (
        P(("patch", "expert"), "hidden"),
        P("expert", None, ("patch", "hidden")),
        P("expert", ("patch", "hidden"), None),
        P("expert", ("patch", "hidden")),
    )
    return jax.shard_map(local, mesh=mesh, in_specs=in_specs, out_specs=out_specs, check_vma=False)
```

```python
import functools

import jax
import jax.numpy as jnp
from jax import lax
from jax.experimental import pallas as pl
from jax.experimental.pallas import tpu as pltpu
from jax.sharding import PartitionSpec as P

inv_root_two = 0.7071067811865476
inv_root_two_pi = 0.3989422804014327


def gelu_parts(pre):
    normal_cdf = 0.5 * (1.0 + lax.erf(pre * inv_root_two))
    density = jnp.exp(-0.5 * pre * pre) * inv_root_two_pi
    return (pre * normal_cdf, normal_cdf + pre * density)


def general(tokens, cotangent, w_in, w_out, gates, picks, counts):
    tok_dev, width = tokens.shape
    patch_count = lax.axis_size("patch")
    expert_count = lax.axis_size("expert")
    hidden_parts = lax.axis_size("hidden")
    capacity = picks.shape[1]
    slots = capacity // patch_count
    sources = patch_count * expert_count
    bound = 2 * max(1, slots // sources)
    limit = sources * bound
    patch_here = lax.axis_index("patch")
    expert_here = lax.axis_index("expert")
    source_here = patch_here * expert_count + expert_here
    slot_ids = jnp.arange(capacity, dtype=jnp.int32)
    live = slot_ids[None, :] < counts[:, None]
    holder = picks // tok_dev
    local_row = picks % tok_dev
    mine = (
        ((holder == source_here) & live).reshape(expert_count, patch_count, slots).astype(jnp.int32)
    )
    order_mine = jnp.cumsum(mine, axis=2) - 1
    expert_ids = jnp.arange(expert_count, dtype=jnp.int32)[:, None, None]
    patch_ids = jnp.arange(patch_count, dtype=jnp.int32)[None, :, None]
    position = (patch_ids * expert_count + expert_ids) * bound + order_mine
    position = jnp.where(mine == 1, position, limit)
    send_table = (
        jnp.full((limit,), tok_dev, jnp.int32)
        .at[position.reshape(-1)]
        .set(local_row.reshape(-1), mode="drop")
    )
    send_rows = jnp.take(tokens, send_table, axis=0, mode="fill", fill_value=0).reshape(
        sources, bound, width
    )
    send_grads = jnp.take(cotangent, send_table, axis=0, mode="fill", fill_value=0).reshape(
        sources, bound, width
    )
    came_rows, came_grads = (
        lax.all_to_all(send_rows, ("patch", "expert"), split_axis=0, concat_axis=0, tiled=True),
        lax.all_to_all(send_grads, ("patch", "expert"), split_axis=0, concat_axis=0, tiled=True),
    )
    my_picks = lax.dynamic_slice_in_dim(picks, expert_here, 1, 0)[0]
    block_picks = lax.dynamic_slice_in_dim(my_picks, patch_here * slots, slots, 0)
    count_here = lax.dynamic_slice_in_dim(counts, expert_here, 1, 0)[0]
    within = jnp.arange(slots, dtype=jnp.int32)
    block_live = patch_here * slots + within < count_here
    block_holder = block_picks // tok_dev
    earlier_same = (
        (block_holder[:, None] == block_holder[None, :])
        & block_live[None, :]
        & (within[None, :] < within[:, None])
    )
    block_order = jnp.sum(earlier_same.astype(jnp.int32), axis=1)
    came_index = jnp.where(block_live, block_holder * bound + block_order, limit)
    block_rows = jnp.take(
        came_rows.reshape(limit, width), came_index, axis=0, mode="fill", fill_value=0
    )
    block_grads = jnp.take(
        came_grads.reshape(limit, width), came_index, axis=0, mode="fill", fill_value=0
    )
    slot_rows, grad_rows = (
        lax.all_gather(block_rows, "patch", axis=0, tiled=True),
        lax.all_gather(block_grads, "patch", axis=0, tiled=True),
    )
    gate_col = gates[0][:, None]
    weight_in = w_in[0]
    weight_out = w_out[0]
    unit_count = weight_in.shape[1]
    pre = jnp.dot(slot_rows, weight_in, preferred_element_type=jnp.float32)
    act, slope = gelu_parts(pre)
    act_b = act.astype(jnp.bfloat16)
    back_act = lax.dot_general(
        grad_rows, weight_out, (((1,), (1,)), ((), ())), preferred_element_type=jnp.float32
    )
    gate_grad = jnp.sum(act * back_act, axis=1)
    back_pre = (gate_col * back_act * slope).astype(jnp.bfloat16)
    gated_rows = (gate_col * grad_rows.astype(jnp.float32)).astype(jnp.bfloat16)
    grad_in = lax.dot_general(
        slot_rows, back_pre, (((0,), (0,)), ((), ())), preferred_element_type=jnp.float32
    )
    grad_out = lax.dot_general(
        act_b, gated_rows, (((0,), (0,)), ((), ())), preferred_element_type=jnp.float32
    )
    gate_terms = gate_grad.reshape(patch_count * hidden_parts, slots // hidden_parts)
    d_gates = lax.psum_scatter(gate_terms, ("patch", "hidden"), scatter_dimension=0, tiled=True)
    selector = (jnp.arange(tok_dev, dtype=jnp.int32)[:, None] == send_table[None, :]).astype(
        jnp.bfloat16
    )
    back_blocks = back_pre.reshape(patch_count, slots, unit_count)
    weight_halves = weight_in.reshape(hidden_parts, width // hidden_parts, unit_count)
    slot_terms = jnp.einsum(
        "psf,hdf->phsd", back_blocks, weight_halves, preferred_element_type=jnp.float32
    ).astype(jnp.bfloat16)
    slot_terms = slot_terms.reshape(patch_count * hidden_parts, slots, width // hidden_parts)
    slot_sum = lax.psum_scatter(
        slot_terms, ("patch", "hidden"), scatter_dimension=0, tiled=True
    ).astype(jnp.float32)[0]
    slot_grad = slot_sum.astype(jnp.bfloat16)
    going_back = (
        jnp.zeros((limit, width // hidden_parts), jnp.bfloat16)
        .at[came_index]
        .set(slot_grad, mode="drop")
    )
    send_width = width // hidden_parts
    returned = lax.all_to_all(
        going_back.reshape(sources, bound, send_width),
        ("patch", "expert"),
        split_axis=0,
        concat_axis=0,
        tiled=True,
    )
    returned = returned.reshape(limit, send_width)
    token_grad = jnp.dot(selector, returned, preferred_element_type=jnp.float32)
    d_tokens = token_grad.astype(jnp.bfloat16)
    return (
        d_tokens,
        grad_in.astype(jnp.bfloat16)[None],
        grad_out.astype(jnp.bfloat16)[None],
        d_gates,
    )


MESH = pl.DeviceIdType.MESH
f32 = jnp.float32
bf16 = jnp.bfloat16
i32 = jnp.int32
PAIR = 16
PIECES = 4
CAP = 128
HALF = CAP // 2
SPILL = 32
FULL = 128


def contract(a, b, dim_a, dim_b):
    return lax.dot_general(a, b, (((dim_a,), (dim_b,)), ((), ())), preferred_element_type=f32)


def marks(mask):
    return jnp.where(mask, 1.0, 0.0).astype(bf16)


def iota(shape, dim):
    return lax.broadcasted_iota(i32, shape, dim)


def split_three(x):
    a = x.astype(bf16)
    rest = x - a.astype(f32)
    b = rest.astype(bf16)
    return (a, b, (rest - b.astype(f32)).astype(bf16))


def row_sums(x):
    ones = jnp.ones((8, x.shape[1]), bf16)
    return sum(contract(ones, part, 1, 1) for part in split_three(x))[0:1]


def previous(x):
    return pltpu.roll(x, 1, 0)


def following(x):
    return pltpu.roll(x, x.shape[0] - 1, 0)


def kernel(
    planes,
    experts,
    tokens,
    cotangent,
    w_in_hbm,
    w_out_hbm,
    gates,
    picks,
    counts,
    d_tok_hbm,
    d_in_hbm,
    d_out_hbm,
    d_gates,
    misfit,
    codes,
    taken,
    meta,
    tables,
    offs,
    lens,
    pick_sel,
    pack_sel,
    spill_sel,
    held,
    going,
    came,
    spilled,
    allrows,
    win,
    wout,
    act_s,
    back_s,
    home,
    part_out,
    part_in,
    sum_out,
    sum_in,
    grad_go,
    grad_came,
    grad_ret,
    d_tok,
    d_in,
    d_out,
    gate_lo,
    gate_hi,
    gate_all,
    load_sem,
    go_send,
    go_recv,
    spill_send,
    spill_recv,
    ring_send,
    ring_recv,
    twin_send,
    twin_recv,
    part_send,
    part_recv,
    sum_send,
    sum_recv,
    ret_send,
    ret_recv,
    grad_send,
    grad_recv,
    gate_send,
    gate_recv,
    store_sem,
):
    z = lax.axis_index("patch")
    e = lax.axis_index("expert")
    c = lax.axis_index("hidden")
    other = 1 - c
    up = (lax.rem(z + 1, planes), e, c)
    down = (lax.rem(z + planes - 1, planes), e, c)
    twin = (z, e, other)
    piece = held.shape[3]
    pairs = experts * PAIR
    capacity = codes.shape[1]
    plane_peers = [(z, lax.rem(e + k, experts), c) for k in range(1, experts)]
    me = z * 2 + c
    column_ids = [lax.rem(me + k, 2 * planes) for k in range(1, 2 * planes)]
    column_peers = [(i // 2, e, lax.rem(i, 2)) for i in column_ids]

    barrier = pltpu.get_barrier_semaphore()
    for peer in plane_peers + column_peers:
        pl.semaphore_signal(barrier, inc=1, device_id=peer, device_id_type=MESH)

    loads = []
    for a, ref in enumerate((tokens, cotangent)):
        for j in range(2):
            col = pl.multiple_of((2 * c + j) * piece, piece)
            cp = pltpu.make_async_copy(
                ref.at[:, pl.ds(col, piece)], held.at[a, j], load_sem.at[2 * a + j]
            )
            cp.start()
            loads.append(cp)
    load_in = pltpu.make_async_copy(w_in_hbm, win, load_sem.at[4])
    load_out = pltpu.make_async_copy(w_out_hbm, wout, load_sem.at[5])
    load_in.start()
    load_out.start()

    before = marks(iota((FULL, FULL), 0) < iota((FULL, FULL), 1))
    place = iota((1, capacity), 1)
    for i in range(experts):
        codes[i : i + 1, :] = jnp.where(place < counts[i], picks[i : i + 1, :], -1)
    base = (z * experts + e) * FULL
    wanted = iota((FULL, capacity), 0) + base

    def find(i, carry):
        match = jnp.where(codes[pl.ds(i, 1), :] == wanted, 1.0, 0.0)
        folded = match[:, 0:FULL]
        for k in range(1, capacity // FULL):
            folded += match[:, k * FULL : (k + 1) * FULL]
        taken[pl.ds(i, 1), :] = contract(jnp.ones((8, FULL), bf16), folded.astype(bf16), 1, 1)[0:1]
        return carry

    lax.fori_loop(0, experts, find, 0)
    present = taken[...]
    order = contract(present.astype(bf16), before, 1, 0)
    order = jnp.where(present > 0.5, order, -1.0).astype(i32)
    for i in range(experts):
        pick_sel[i * PAIR : (i + 1) * PAIR, :] = marks(
            iota((PAIR, FULL), 0) == order[i : i + 1, :]
        )

    pl.semaphore_wait(barrier, len(plane_peers) + len(column_peers))

    def remote(src, dst, s, r, dev):
        return pltpu.make_async_remote_copy(
            src_ref=src, dst_ref=dst, send_sem=s, recv_sem=r, device_id=dev, device_id_type=MESH
        )

    own_rows = pl.ds(pl.multiple_of(e * PAIR, PAIR), PAIR)

    def plane_copy(src, dst, ssem, rsem, k):
        to = pl.multiple_of(lax.rem(e + k, experts) * PAIR, PAIR)
        return remote(
            src.at[pl.ds(to, PAIR)], dst.at[own_rows], ssem.at[k], rsem.at[k], plane_peers[k - 1]
        )

    def go_copy(a, j, k):
        return plane_copy(
            going.at[a, j], came.at[a, j], go_send.at[a, j], go_recv.at[a, j], k
        )

    def grad_copy(j, k):
        return plane_copy(
            grad_go.at[j], grad_came.at[j], grad_send.at[j], grad_recv.at[j], k
        )

    def spill_up(a, j):
        return remote(
            spilled.at[a, j, pl.ds(0, SPILL)],
            came.at[a, j, pl.ds(pairs, SPILL)],
            spill_send.at[0, a, j],
            spill_recv.at[0, a, j],
            up,
        )

    def spill_down(a, j):
        return remote(
            spilled.at[a, j, pl.ds(SPILL, SPILL)],
            came.at[a, j, pl.ds(pairs + SPILL, SPILL)],
            spill_send.at[1, a, j],
            spill_recv.at[1, a, j],
            down,
        )

    def ret_down(j):
        return remote(
            grad_go.at[j, pl.ds(pairs, SPILL)],
            grad_ret.at[j, pl.ds(0, SPILL)],
            ret_send.at[0, j],
            ret_recv.at[0, j],
            down,
        )

    def ret_up(j):
        return remote(
            grad_go.at[j, pl.ds(pairs + SPILL, SPILL)],
            grad_ret.at[j, pl.ds(SPILL, SPILL)],
            ret_send.at[1, j],
            ret_recv.at[1, j],
            up,
        )

    def ring_up(a, j, t):
        q = 2 * c + j
        return remote(
            allrows.at[a, q, t, pl.ds(0, HALF)],
            allrows.at[a, q, t + 1, pl.ds(0, HALF)],
            ring_send.at[0, a, j, t],
            ring_recv.at[0, a, j, t + 1],
            up,
        )

    def ring_down(a, j, t):
        q = 2 * c + j
        return remote(
            allrows.at[a, q, t, pl.ds(HALF, HALF)],
            allrows.at[a, q, t + 1, pl.ds(HALF, HALF)],
            ring_send.at[1, a, j, t],
            ring_recv.at[1, a, j, t + 1],
            down,
        )

    def twin_copy(a, j, t):
        q = 2 * c + j
        return remote(
            allrows.at[a, q, t],
            allrows.at[a, q, t],
            twin_send.at[a, j, t],
            twin_recv.at[a, j, t],
            twin,
        )

    def part_copy(j, t):
        slot = lax.rem(t, 2)
        return remote(
            part_out.at[slot, j], part_in.at[t, j], part_send.at[t, j], part_recv.at[t, j], twin
        )

    def sum_up(j, t):
        return remote(
            sum_out.at[lax.rem(t, 2), j, pl.ds(0, HALF)],
            sum_in.at[t, j, pl.ds(0, HALF)],
            sum_send.at[0, j, t],
            sum_recv.at[0, j, t],
            up,
        )

    def sum_down(j, t):
        return remote(
            sum_out.at[lax.rem(t, 2), j, pl.ds(HALF, HALF)],
            sum_in.at[t, j, pl.ds(HALF, HALF)],
            sum_send.at[1, j, t],
            sum_recv.at[1, j, t],
            down,
        )

    for a in range(2):
        for j in range(2):
            loads[2 * a + j].wait()
            going[a, j] = contract(pick_sel[...], held[a, j], 1, 0).astype(bf16)
            came[a, j, own_rows, :] = going[a, j, own_rows, :]
            for k in range(1, experts):
                go_copy(a, j, k).start()

    mine = codes[pl.ds(e, 1), :]
    by_holder = marks((mine >> 7) == iota((FULL, capacity), 0))
    by_row = marks((mine & (FULL - 1)) == iota((FULL, capacity), 0))
    chosen = contract(by_holder, by_row, 1, 1).astype(bf16)
    ranks = contract(chosen, before, 1, 0)
    sizes = contract(chosen, jnp.ones((FULL, FULL), bf16), 1, 0)
    sizes_b = sizes.astype(bf16)
    from_s = iota((FULL, FULL), 1)
    to_s = iota((FULL, FULL), 0)
    ahead = marks((from_s // PAIR == to_s // PAIR) & (from_s < to_s))
    offsets = contract(ahead, sizes_b, 1, 0)
    offs[...] = offsets
    lens[...] = sizes
    group_lane = iota((planes, FULL), 1) // PAIR
    group_row = iota((planes, FULL), 0)
    grouped = marks(group_lane == group_row)
    amount = contract(grouped, sizes_b, 1, 0).astype(i32)
    so_far = contract(marks(group_lane <= group_row), sizes_b, 1, 0).astype(i32)
    live = so_far[planes - 1 : planes, :]
    excess = so_far - ((live * (group_row + 1)) >> 3)
    middle = (jnp.max(excess, axis=0, keepdims=True) + jnp.min(excess, axis=0, keepdims=True)) >> 1
    flow = excess - middle
    rising = jnp.maximum(flow, 0)
    sinking = jnp.maximum(-flow, 0)
    risen = previous(rising)
    keep = amount - rising - previous(sinking)
    up_at = following(keep)
    down_at = previous(keep + risen)
    for i, table in enumerate((keep, rising, risen, sinking)):
        tables[i] = table

    def spread(x):
        return contract(grouped, x.astype(bf16), 0, 0)

    keep_s, rising_s = spread(keep), spread(rising)
    dest = offsets + ranks - keep_s
    goes_up = (dest >= 0) & (dest < rising_s)
    goes_down = dest >= rising_s
    spot = jnp.where(
        dest < 0, dest + keep_s, jnp.where(goes_up, spread(up_at) + dest, spread(down_at) + dest - rising_s)
    )
    goes_down = (dest >= 0) & goes_down
    shift = jnp.where(goes_up, 1.0, jnp.where(goes_down, -1.0, 0.0))

    def per_slot(x):
        return jnp.sum(
            contract(x.astype(bf16), by_holder, 0, 0) * by_row.astype(f32), axis=0, keepdims=True
        ).astype(i32)

    slot = per_slot(spot)
    block = ((mine >> 11) + per_slot(shift)) & (planes - 1)
    when = jnp.where(slot < HALF, z - block, block - z) & (planes - 1)
    meta[0:1, :] = jnp.where(mine < 0, -1, when * CAP + slot)
    meta[1:2, :] = block
    meta[2:3, :] = jnp.where(mine < 0, -1, slot)

    own_group = pl.ds(pl.multiple_of(z * PAIR, PAIR), PAIR)
    widen = marks(iota((PAIR, pairs), 1) // PAIR == iota((PAIR, pairs), 0))
    start = contract(offs[own_group, :].astype(bf16), widen, 0, 0).astype(i32)
    size = contract(lens[own_group, :].astype(bf16), widen, 0, 0).astype(i32)
    index = iota((CAP, pairs), 1) & (PAIR - 1)
    spot_here = jnp.where(index < size, start + index, -1)

    def own(i):
        return tables[i, pl.ds(z, 1), :][:, 0:1]

    keep_z, rising_z, risen_z, sinking_z = own(0), own(1), own(2), own(3)
    line = iota((CAP, pairs), 0)
    pack_sel[:, 0:pairs] = marks((spot_here == line) & (line < keep_z))
    lane = iota((CAP, FULL), 1)
    line = iota((CAP, FULL), 0) - keep_z
    pack_sel[:, pairs : pairs + FULL] = marks(
        ((lane < SPILL) & (lane < risen_z) & (line == lane))
        | ((lane >= SPILL) & (lane < SPILL + sinking_z) & (line - risen_z == lane - SPILL))
    )
    line = iota((2 * SPILL, pairs), 0)
    above = spot_here[0 : 2 * SPILL, :] - keep_z
    spill_sel[...] = marks(
        ((line < SPILL) & (line < rising_z) & (above == line))
        | ((line >= SPILL) & (above - rising_z == line - SPILL) & (spot_here[0 : 2 * SPILL, :] >= 0))
    )

    all_codes = codes[...] >> 11
    held_by = [
        jnp.sum(jnp.where(all_codes == i, 1, 0), axis=1, keepdims=True) for i in range(planes)
    ]
    running = [held_by[0]]
    for i in range(1, planes):
        running.append(running[-1] + held_by[i])
    over = [running[i] - ((running[-1] * (i + 1)) >> 3) for i in range(planes)]
    most, least = over[0], over[0]
    for x in over[1:]:
        most, least = jnp.maximum(most, x), jnp.minimum(least, x)
    mid = (most + least) >> 1
    bad = jnp.maximum(most - mid, mid - least) - SPILL
    for i in range(planes):
        leaves = jnp.maximum(over[i] - mid, 0) + jnp.maximum(mid - over[i - 1], 0)
        bad = jnp.maximum(bad, leaves - held_by[i])
    misfit[...] = jnp.broadcast_to(jnp.max(bad, axis=0, keepdims=True), misfit.shape)

    for a in range(2):
        for j in range(2):
            came[a, j, pairs + 2 * SPILL :, :] = jnp.zeros((FULL - 2 * SPILL, piece), bf16)
    for a in range(2):
        for j in range(2):
            for k in range(1, experts):
                go_copy(a, j, k).wait()
            spilled[a, j] = contract(spill_sel[...], came[a, j, 0:pairs, :], 1, 0).astype(bf16)
            spill_up(a, j).start()
            spill_down(a, j).start()
            spill_up(a, j).wait()
            spill_down(a, j).wait()
            allrows[a, 2 * c + j, 0] = contract(pack_sel[...], came[a, j], 1, 0).astype(bf16)
            ring_up(a, j, 0).start()
            ring_down(a, j, 0).start()
            twin_copy(a, j, 0).start()
    load_in.wait()
    load_out.wait()

    def step(t, carry):
        for a in range(2):
            for j in range(2):

                @pl.when(t > 0)
                def _():
                    ring_up(a, j, t - 1).wait_recv()

                    @pl.when(t < planes - 1)
                    def _():
                        ring_up(a, j, t).start()

                    ring_down(a, j, t - 1).wait_recv()

                    @pl.when(t < planes - 1)
                    def _():
                        ring_down(a, j, t).start()

                    twin_copy(a, j, t).start()

        for a in range(2):
            for j in range(2):
                twin_copy(a, j, t).wait_recv()
        pre = contract(allrows[0, 0, t], win[0], 1, 0)
        back = contract(allrows[1, 0, t], wout[:, 0:piece], 1, 1)
        for q in range(1, PIECES):
            pre += contract(allrows[0, q, t], win[q], 1, 0)
            back += contract(allrows[1, q, t], wout[:, q * piece : (q + 1) * piece], 1, 1)
        act, slope = gelu_parts(pre)
        gate = jnp.sum(
            jnp.where(meta[0:1, :] == iota((CAP, capacity), 0) + t * CAP, gates[...], 0.0),
            axis=1,
            keepdims=True,
        )
        act_s[t] = (gate * act).astype(bf16)
        back_pre = (gate * back * slope).astype(bf16)
        back_s[t] = back_pre
        gate_row = row_sums(act * back)
        gate_lo[pl.ds(lax.rem(z + planes - t, planes), 1), :] = gate_row
        gate_hi[pl.ds(lax.rem(z + t, planes), 1), :] = gate_row

        for j in range(2):

            @pl.when(t > 1)
            def _():
                part_copy(j, t - 2).wait_send()

            part_out[lax.rem(t, 2), j] = contract(back_pre, win[2 * other + j], 1, 1).astype(bf16)
            part_copy(j, t).start()
        for j in range(2):
            own_part = contract(back_pre, win[2 * c + j], 1, 1)
            part_copy(j, t).wait_recv()
            own_part += part_in[t, j].astype(f32)

            @pl.when(t == 0)
            def _():
                home[j] = own_part

            @pl.when(t > 2)
            def _():
                sum_up(j, t - 2).wait_send()
                sum_down(j, t - 2).wait_send()

            @pl.when(t > 1)
            def _():
                sum_up(j, t - 1).wait_recv()
                sum_down(j, t - 1).wait_recv()
                sum_out[lax.rem(t, 2), j] = (own_part + sum_in[t - 1, j].astype(f32)).astype(bf16)

            @pl.when(t == 1)
            def _():
                sum_out[lax.rem(t, 2), j] = own_part.astype(bf16)

            @pl.when(t > 0)
            def _():
                sum_up(j, t).start()
                sum_down(j, t).start()

        return carry

    lax.fori_loop(0, planes, step, 0)

    gate_all[me] = jnp.where(iota(gate_lo.shape, 1) < HALF, gate_lo[...], gate_hi[...])

    def gate_copy(k):
        return remote(
            gate_all.at[me], gate_all.at[me], gate_send.at[k], gate_recv.at[k], column_peers[k - 1]
        )

    for k in range(1, 2 * planes):
        gate_copy(k).start()

    rows = planes * CAP
    act_all = act_s[...].reshape(rows, act_s.shape[2])
    for q in range(PIECES):
        d_out[q] = contract(act_all, allrows[1, q].reshape(rows, piece), 0, 0).astype(bf16)

    last = planes - 1
    for j in range(2):
        sum_up(j, last).wait_recv()
        sum_down(j, last).wait_recv()
        slot_grad = (home[j] + sum_in[last, j].astype(f32)).astype(bf16)
        grad_go[j, pairs:, :] = contract(pack_sel[:, pairs:], slot_grad, 0, 0).astype(bf16)
        ret_up(j).start()
        ret_down(j).start()
        grad_go[j, 0:pairs, :] = contract(pack_sel[:, 0:pairs], slot_grad, 0, 0).astype(bf16)
        ret_up(j).wait()
        ret_down(j).wait()
        returned = contract(spill_sel[...], grad_ret[j], 0, 0)
        grad_go[j, 0:pairs, :] = (grad_go[j, 0:pairs, :].astype(f32) + returned).astype(bf16)
        grad_came[j, own_rows, :] = grad_go[j, own_rows, :]
        for k in range(1, experts):
            grad_copy(j, k).start()

    stores = []
    for q in range(PIECES):
        cp = pltpu.make_async_copy(
            d_out.at[q], d_out_hbm.at[:, pl.ds(q * piece, piece)], store_sem.at[q]
        )
        cp.start()
        stores.append(cp)
    back_all = back_s[...].reshape(rows, back_s.shape[2])
    for q in range(PIECES):
        turned = contract(back_all, allrows[0, q].reshape(rows, piece), 0, 0)
        d_in[q] = turned.T.astype(bf16)
        cp = pltpu.make_async_copy(d_in.at[q], d_in_hbm.at[q], store_sem.at[PIECES + q])
        cp.start()
        stores.append(cp)

    for k in range(1, 2 * planes):
        gate_copy(k).wait()
    total = gate_all[0]
    for i in range(1, 2 * planes):
        total += gate_all[i]
    own_lanes = pl.ds(pl.multiple_of(z * CAP, CAP), CAP)
    found = marks(meta[2:3, own_lanes] == iota((CAP, CAP), 0))
    values = sum(contract(part, found, 1, 0) for part in split_three(total))
    values = jnp.sum(
        jnp.where(meta[1:2, own_lanes] == iota(values.shape, 0), values, 0.0),
        axis=0,
        keepdims=True,
    )
    d_gates[...] = jnp.where(c == 0, values[:, 0:HALF], values[:, HALF:])

    for j in range(2):
        for k in range(1, experts):
            grad_copy(j, k).wait()
        d_tok[j] = contract(pick_sel[...], grad_came[j], 0, 0).astype(bf16)
        cp = pltpu.make_async_copy(
            d_tok.at[j], d_tok_hbm.at[:, pl.ds(j * piece, piece)], store_sem.at[2 * PIECES + j]
        )
        cp.start()
        stores.append(cp)

    for a in range(2):
        for j in range(2):
            for t in range(planes):
                twin_copy(a, j, t).wait_send()
                if t < planes - 1:
                    ring_up(a, j, t).wait_send()
                    ring_down(a, j, t).wait_send()
    for j in range(2):
        for t in (planes - 2, planes - 1):
            part_copy(j, t).wait_send()
            sum_up(j, t).wait_send()
            sum_down(j, t).wait_send()
    for cp in stores:
        cp.wait()


def fast(tokens, cotangent, w_in, w_out, gates, picks, counts):
    planes = lax.axis_size("patch")
    experts = lax.axis_size("expert")
    tok_dev, width = tokens.shape
    units = w_in.shape[2]
    capacity = picks.shape[1]
    piece = width // PIECES
    pairs = experts * PAIR
    vmem = pl.BlockSpec(memory_space=pltpu.VMEM)
    smem = pl.BlockSpec(memory_space=pltpu.SMEM)
    hbm = pl.BlockSpec(memory_space=pl.ANY)
    dma = pltpu.SemaphoreType.DMA
    scratch = [
        pltpu.VMEM((experts, capacity), i32),
        pltpu.VMEM((experts, tok_dev), f32),
        pltpu.VMEM((8, capacity), i32),
        pltpu.VMEM((4, planes, FULL), i32),
        pltpu.VMEM((FULL, FULL), f32),
        pltpu.VMEM((FULL, FULL), f32),
        pltpu.VMEM((pairs, tok_dev), bf16),
        pltpu.VMEM((CAP, pairs + FULL), bf16),
        pltpu.VMEM((2 * SPILL, pairs), bf16),
        pltpu.VMEM((2, 2, tok_dev, piece), bf16),
        pltpu.VMEM((2, 2, pairs, piece), bf16),
        pltpu.VMEM((2, 2, pairs + FULL, piece), bf16),
        pltpu.VMEM((2, 2, 2 * SPILL, piece), bf16),
        pltpu.VMEM((2, PIECES, planes, CAP, piece), bf16),
        pltpu.VMEM((PIECES, piece, units), bf16),
        pltpu.VMEM((units, width), bf16),
        pltpu.VMEM((planes, CAP, units), bf16),
        pltpu.VMEM((planes, CAP, units), bf16),
        pltpu.VMEM((2, CAP, piece), f32),
        pltpu.VMEM((2, 2, CAP, piece), bf16),
        pltpu.VMEM((planes, 2, CAP, piece), bf16),
        pltpu.VMEM((2, 2, CAP, piece), bf16),
        pltpu.VMEM((planes, 2, CAP, piece), bf16),
        pltpu.VMEM((2, pairs + FULL, piece), bf16),
        pltpu.VMEM((2, pairs, piece), bf16),
        pltpu.VMEM((2, 2 * SPILL, piece), bf16),
        pltpu.VMEM((2, tok_dev, piece), bf16),
        pltpu.VMEM((PIECES, piece, units), bf16),
        pltpu.VMEM((PIECES, units, piece), bf16),
        pltpu.VMEM((planes, CAP), f32),
        pltpu.VMEM((planes, CAP), f32),
        pltpu.VMEM((2 * planes, planes, CAP), f32),
        dma((6,)),
        dma((2, 2, experts)),
        dma((2, 2, experts)),
        dma((2, 2, 2)),
        dma((2, 2, 2)),
        dma((2, 2, 2, planes)),
        dma((2, 2, 2, planes)),
        dma((2, 2, planes)),
        dma((2, 2, planes)),
        dma((planes, 2)),
        dma((planes, 2)),
        dma((2, 2, planes)),
        dma((2, 2, planes)),
        dma((2, 2)),
        dma((2, 2)),
        dma((2, experts)),
        dma((2, experts)),
        dma((2 * planes,)),
        dma((2 * planes,)),
        dma((2 * PIECES + 2,)),
    ]
    d_tokens, d_in, d_out, d_gates, misfit = pl.pallas_call(
        functools.partial(kernel, planes, experts),
        out_shape=(
            jax.ShapeDtypeStruct((tok_dev, width // 2), bf16),
            jax.ShapeDtypeStruct((PIECES, piece, units), bf16),
            jax.ShapeDtypeStruct((units, width), bf16),
            jax.ShapeDtypeStruct((1, HALF), f32),
            jax.ShapeDtypeStruct((8, FULL), i32),
        ),
        in_specs=[hbm, hbm, hbm, hbm, vmem, vmem, smem],
        out_specs=(hbm, hbm, hbm, vmem, vmem),
        scratch_shapes=scratch,
        compiler_params=pltpu.CompilerParams(
            collective_id=0, has_side_effects=True, vmem_limit_bytes=60 * 2**20
        ),
    )(tokens, cotangent, w_in.reshape(PIECES, piece, units), w_out[0], gates, picks, counts)
    return (d_tokens, d_in.reshape(w_in.shape), d_out[None], d_gates, misfit)


def local(*args):
    results = fast(*args)
    return lax.cond(
        results[4][0, 0] <= 0, lambda found, args: found, lambda found, args: general(*args), results[:4], args
    )


def solution(mesh):
    in_specs = (
        P(("patch", "expert"), None),
        P(("patch", "expert"), None),
        P("expert", None, ("patch", "hidden")),
        P("expert", ("patch", "hidden"), None),
        P("expert", None),
        P(),
        P(),
    )
    out_specs = (
        P(("patch", "expert"), "hidden"),
        P("expert", None, ("patch", "hidden")),
        P("expert", ("patch", "hidden"), None),
        P("expert", ("patch", "hidden")),
    )
    return jax.shard_map(local, mesh=mesh, in_specs=in_specs, out_specs=out_specs, check_vma=False)
```

```python
import functools

import jax
import jax.numpy as jnp
from jax import lax
from jax.experimental import pallas as pl
from jax.experimental.pallas import tpu as pltpu
from jax.sharding import PartitionSpec as P

inv_root_two = 0.7071067811865476
inv_root_two_pi = 0.3989422804014327


def gelu_parts(pre):
    normal_cdf = 0.5 * (1.0 + lax.erf(pre * inv_root_two))
    density = jnp.exp(-0.5 * pre * pre) * inv_root_two_pi
    return (pre * normal_cdf, normal_cdf + pre * density)


def general(tokens, cotangent, w_in, w_out, gates, picks, counts):
    tok_dev, width = tokens.shape
    patch_count = lax.axis_size("patch")
    expert_count = lax.axis_size("expert")
    hidden_parts = lax.axis_size("hidden")
    capacity = picks.shape[1]
    slots = capacity // patch_count
    sources = patch_count * expert_count
    bound = 2 * max(1, slots // sources)
    limit = sources * bound
    patch_here = lax.axis_index("patch")
    expert_here = lax.axis_index("expert")
    source_here = patch_here * expert_count + expert_here
    slot_ids = jnp.arange(capacity, dtype=jnp.int32)
    live = slot_ids[None, :] < counts[:, None]
    holder = picks // tok_dev
    local_row = picks % tok_dev
    mine = (
        ((holder == source_here) & live).reshape(expert_count, patch_count, slots).astype(jnp.int32)
    )
    order_mine = jnp.cumsum(mine, axis=2) - 1
    expert_ids = jnp.arange(expert_count, dtype=jnp.int32)[:, None, None]
    patch_ids = jnp.arange(patch_count, dtype=jnp.int32)[None, :, None]
    position = (patch_ids * expert_count + expert_ids) * bound + order_mine
    position = jnp.where(mine == 1, position, limit)
    send_table = (
        jnp.full((limit,), tok_dev, jnp.int32)
        .at[position.reshape(-1)]
        .set(local_row.reshape(-1), mode="drop")
    )
    send_rows = jnp.take(tokens, send_table, axis=0, mode="fill", fill_value=0).reshape(
        sources, bound, width
    )
    send_grads = jnp.take(cotangent, send_table, axis=0, mode="fill", fill_value=0).reshape(
        sources, bound, width
    )
    came_rows, came_grads = (
        lax.all_to_all(send_rows, ("patch", "expert"), split_axis=0, concat_axis=0, tiled=True),
        lax.all_to_all(send_grads, ("patch", "expert"), split_axis=0, concat_axis=0, tiled=True),
    )
    my_picks = lax.dynamic_slice_in_dim(picks, expert_here, 1, 0)[0]
    block_picks = lax.dynamic_slice_in_dim(my_picks, patch_here * slots, slots, 0)
    count_here = lax.dynamic_slice_in_dim(counts, expert_here, 1, 0)[0]
    within = jnp.arange(slots, dtype=jnp.int32)
    block_live = patch_here * slots + within < count_here
    block_holder = block_picks // tok_dev
    earlier_same = (
        (block_holder[:, None] == block_holder[None, :])
        & block_live[None, :]
        & (within[None, :] < within[:, None])
    )
    block_order = jnp.sum(earlier_same.astype(jnp.int32), axis=1)
    came_index = jnp.where(block_live, block_holder * bound + block_order, limit)
    block_rows = jnp.take(
        came_rows.reshape(limit, width), came_index, axis=0, mode="fill", fill_value=0
    )
    block_grads = jnp.take(
        came_grads.reshape(limit, width), came_index, axis=0, mode="fill", fill_value=0
    )
    slot_rows, grad_rows = (
        lax.all_gather(block_rows, "patch", axis=0, tiled=True),
        lax.all_gather(block_grads, "patch", axis=0, tiled=True),
    )
    gate_col = gates[0][:, None]
    weight_in = w_in[0]
    weight_out = w_out[0]
    unit_count = weight_in.shape[1]
    pre = jnp.dot(slot_rows, weight_in, preferred_element_type=jnp.float32)
    act, slope = gelu_parts(pre)
    act_b = act.astype(jnp.bfloat16)
    back_act = lax.dot_general(
        grad_rows, weight_out, (((1,), (1,)), ((), ())), preferred_element_type=jnp.float32
    )
    gate_grad = jnp.sum(act * back_act, axis=1)
    back_pre = (gate_col * back_act * slope).astype(jnp.bfloat16)
    gated_rows = (gate_col * grad_rows.astype(jnp.float32)).astype(jnp.bfloat16)
    grad_in = lax.dot_general(
        slot_rows, back_pre, (((0,), (0,)), ((), ())), preferred_element_type=jnp.float32
    )
    grad_out = lax.dot_general(
        act_b, gated_rows, (((0,), (0,)), ((), ())), preferred_element_type=jnp.float32
    )
    gate_terms = gate_grad.reshape(patch_count * hidden_parts, slots // hidden_parts)
    d_gates = lax.psum_scatter(gate_terms, ("patch", "hidden"), scatter_dimension=0, tiled=True)
    selector = (jnp.arange(tok_dev, dtype=jnp.int32)[:, None] == send_table[None, :]).astype(
        jnp.bfloat16
    )
    back_blocks = back_pre.reshape(patch_count, slots, unit_count)
    weight_halves = weight_in.reshape(hidden_parts, width // hidden_parts, unit_count)
    slot_terms = jnp.einsum(
        "psf,hdf->phsd", back_blocks, weight_halves, preferred_element_type=jnp.float32
    ).astype(jnp.bfloat16)
    slot_terms = slot_terms.reshape(patch_count * hidden_parts, slots, width // hidden_parts)
    slot_sum = lax.psum_scatter(
        slot_terms, ("patch", "hidden"), scatter_dimension=0, tiled=True
    ).astype(jnp.float32)[0]
    slot_grad = slot_sum.astype(jnp.bfloat16)
    going_back = (
        jnp.zeros((limit, width // hidden_parts), jnp.bfloat16)
        .at[came_index]
        .set(slot_grad, mode="drop")
    )
    send_width = width // hidden_parts
    returned = lax.all_to_all(
        going_back.reshape(sources, bound, send_width),
        ("patch", "expert"),
        split_axis=0,
        concat_axis=0,
        tiled=True,
    )
    returned = returned.reshape(limit, send_width)
    token_grad = jnp.dot(selector, returned, preferred_element_type=jnp.float32)
    d_tokens = token_grad.astype(jnp.bfloat16)
    return (
        d_tokens,
        grad_in.astype(jnp.bfloat16)[None],
        grad_out.astype(jnp.bfloat16)[None],
        d_gates,
    )


MESH = pl.DeviceIdType.MESH
f32 = jnp.float32
bf16 = jnp.bfloat16
i32 = jnp.int32
PAIR = 16
PIECES = 4
CAP = 128
HALF = CAP // 2
SPILL = 32
FULL = 128


def contract(a, b, dim_a, dim_b):
    return lax.dot_general(a, b, (((dim_a,), (dim_b,)), ((), ())), preferred_element_type=f32)


def marks(mask):
    return jnp.where(mask, 1.0, 0.0).astype(bf16)


def iota(shape, dim):
    return lax.broadcasted_iota(i32, shape, dim)


def split_three(x):
    a = x.astype(bf16)
    rest = x - a.astype(f32)
    b = rest.astype(bf16)
    return (a, b, (rest - b.astype(f32)).astype(bf16))


def row_sums(x):
    ones = jnp.ones((8, x.shape[1]), bf16)
    return sum(contract(ones, part, 1, 1) for part in split_three(x))[0:1]


def previous(x):
    return pltpu.roll(x, 1, 0)


def following(x):
    return pltpu.roll(x, x.shape[0] - 1, 0)


def kernel(
    planes,
    experts,
    tokens,
    cotangent,
    w_in_hbm,
    w_out_hbm,
    gates,
    picks,
    counts,
    d_tok_hbm,
    d_in_hbm,
    d_out_hbm,
    d_gates,
    misfit,
    codes,
    taken,
    meta,
    tables,
    offs,
    lens,
    pick_sel,
    pack_sel,
    spill_sel,
    held,
    going,
    came,
    spilled,
    allrows,
    win,
    wout,
    act_s,
    back_s,
    home,
    part_out,
    part_in,
    sum_out,
    sum_in,
    grad_go,
    grad_came,
    grad_ret,
    d_tok,
    d_in,
    d_out,
    gate_lo,
    gate_hi,
    gate_all,
    load_sem,
    go_send,
    go_recv,
    spill_send,
    spill_recv,
    ring_send,
    ring_recv,
    twin_send,
    twin_recv,
    part_send,
    part_recv,
    sum_send,
    sum_recv,
    ret_send,
    ret_recv,
    grad_send,
    grad_recv,
    gate_send,
    gate_recv,
    store_sem,
):
    z = lax.axis_index("patch")
    e = lax.axis_index("expert")
    c = lax.axis_index("hidden")
    other = 1 - c
    up = (lax.rem(z + 1, planes), e, c)
    down = (lax.rem(z + planes - 1, planes), e, c)
    twin = (z, e, other)
    piece = held.shape[3]
    pairs = experts * PAIR
    capacity = codes.shape[1]
    plane_peers = [(z, lax.rem(e + k, experts), c) for k in range(1, experts)]
    me = z * 2 + c
    column_ids = [lax.rem(me + k, 2 * planes) for k in range(1, 2 * planes)]
    column_peers = [(i // 2, e, lax.rem(i, 2)) for i in column_ids]

    barrier = pltpu.get_barrier_semaphore()
    for peer in plane_peers + column_peers:
        pl.semaphore_signal(barrier, inc=1, device_id=peer, device_id_type=MESH)

    loads = []
    for a, ref in enumerate((tokens, cotangent)):
        for j in range(2):
            col = pl.multiple_of((2 * c + j) * piece, piece)
            cp = pltpu.make_async_copy(
                ref.at[:, pl.ds(col, piece)], held.at[a, j], load_sem.at[2 * a + j]
            )
            cp.start()
            loads.append(cp)
    load_in = pltpu.make_async_copy(w_in_hbm, win, load_sem.at[4])
    load_out = pltpu.make_async_copy(w_out_hbm, wout, load_sem.at[5])
    load_in.start()
    load_out.start()

    before = marks(iota((FULL, FULL), 0) < iota((FULL, FULL), 1))
    place = iota((1, capacity), 1)
    for i in range(experts):
        codes[i : i + 1, :] = jnp.where(place < counts[i], picks[i : i + 1, :], -1)
    base = (z * experts + e) * FULL
    wanted = iota((FULL, capacity), 0) + base

    def find(i, carry):
        match = jnp.where(codes[pl.ds(i, 1), :] == wanted, 1.0, 0.0)
        folded = match[:, 0:FULL]
        for k in range(1, capacity // FULL):
            folded += match[:, k * FULL : (k + 1) * FULL]
        taken[pl.ds(i, 1), :] = contract(jnp.ones((8, FULL), bf16), folded.astype(bf16), 1, 1)[0:1]
        return carry

    lax.fori_loop(0, experts, find, 0)
    present = taken[...]
    order = contract(present.astype(bf16), before, 1, 0)
    order = jnp.where(present > 0.5, order, -1.0).astype(i32)
    for i in range(experts):
        pick_sel[i * PAIR : (i + 1) * PAIR, :] = marks(
            iota((PAIR, FULL), 0) == order[i : i + 1, :]
        )

    pl.semaphore_wait(barrier, len(plane_peers) + len(column_peers))

    def remote(src, dst, s, r, dev):
        return pltpu.make_async_remote_copy(
            src_ref=src, dst_ref=dst, send_sem=s, recv_sem=r, device_id=dev, device_id_type=MESH
        )

    own_rows = pl.ds(pl.multiple_of(e * PAIR, PAIR), PAIR)

    def plane_copy(src, dst, ssem, rsem, k):
        to = pl.multiple_of(lax.rem(e + k, experts) * PAIR, PAIR)
        return remote(
            src.at[pl.ds(to, PAIR)], dst.at[own_rows], ssem.at[k], rsem.at[k], plane_peers[k - 1]
        )

    def go_copy(a, j, k):
        return plane_copy(
            going.at[a, j], came.at[a, j], go_send.at[a, j], go_recv.at[a, j], k
        )

    def grad_copy(j, k):
        return plane_copy(
            grad_go.at[j], grad_came.at[j], grad_send.at[j], grad_recv.at[j], k
        )

    def spill_up(a, j):
        return remote(
            spilled.at[a, j, pl.ds(0, SPILL)],
            came.at[a, j, pl.ds(pairs, SPILL)],
            spill_send.at[0, a, j],
            spill_recv.at[0, a, j],
            up,
        )

    def spill_down(a, j):
        return remote(
            spilled.at[a, j, pl.ds(SPILL, SPILL)],
            came.at[a, j, pl.ds(pairs + SPILL, SPILL)],
            spill_send.at[1, a, j],
            spill_recv.at[1, a, j],
            down,
        )

    def ret_down(j):
        return remote(
            grad_go.at[j, pl.ds(pairs, SPILL)],
            grad_ret.at[j, pl.ds(0, SPILL)],
            ret_send.at[0, j],
            ret_recv.at[0, j],
            down,
        )

    def ret_up(j):
        return remote(
            grad_go.at[j, pl.ds(pairs + SPILL, SPILL)],
            grad_ret.at[j, pl.ds(SPILL, SPILL)],
            ret_send.at[1, j],
            ret_recv.at[1, j],
            up,
        )

    def ring_up(a, j, t):
        q = 2 * c + j
        return remote(
            allrows.at[a, q, t, pl.ds(0, HALF)],
            allrows.at[a, q, t + 1, pl.ds(0, HALF)],
            ring_send.at[0, a, j, t],
            ring_recv.at[0, a, j, t + 1],
            up,
        )

    def ring_down(a, j, t):
        q = 2 * c + j
        return remote(
            allrows.at[a, q, t, pl.ds(HALF, HALF)],
            allrows.at[a, q, t + 1, pl.ds(HALF, HALF)],
            ring_send.at[1, a, j, t],
            ring_recv.at[1, a, j, t + 1],
            down,
        )

    def twin_copy(a, j, t):
        q = 2 * c + j
        return remote(
            allrows.at[a, q, t],
            allrows.at[a, q, t],
            twin_send.at[a, j, t],
            twin_recv.at[a, j, t],
            twin,
        )

    def part_copy(j, t):
        slot = lax.rem(t, 2)
        return remote(
            part_out.at[slot, j], part_in.at[t, j], part_send.at[t, j], part_recv.at[t, j], twin
        )

    def sum_up(j, t):
        return remote(
            sum_out.at[lax.rem(t, 2), j, pl.ds(0, HALF)],
            sum_in.at[t, j, pl.ds(0, HALF)],
            sum_send.at[0, j, t],
            sum_recv.at[0, j, t],
            up,
        )

    def sum_down(j, t):
        return remote(
            sum_out.at[lax.rem(t, 2), j, pl.ds(HALF, HALF)],
            sum_in.at[t, j, pl.ds(HALF, HALF)],
            sum_send.at[1, j, t],
            sum_recv.at[1, j, t],
            down,
        )

    for a in range(2):
        for j in range(2):
            loads[2 * a + j].wait()
            going[a, j] = contract(pick_sel[...], held[a, j], 1, 0).astype(bf16)
            came[a, j, own_rows, :] = going[a, j, own_rows, :]
            for k in range(1, experts):
                go_copy(a, j, k).start()

    def forward(p, t):
        a, j = p // 2, p % 2

        @pl.when(t < planes)
        def _():
            ring_up(a, j, t - 1).wait_recv()

            @pl.when(t < planes - 1)
            def _():
                ring_up(a, j, t).start()

            ring_down(a, j, t - 1).wait_recv()

            @pl.when(t < planes - 1)
            def _():
                ring_down(a, j, t).start()

            twin_copy(a, j, t).start()

    mine = codes[pl.ds(e, 1), :]
    by_holder = marks((mine >> 7) == iota((FULL, capacity), 0))
    by_row = marks((mine & (FULL - 1)) == iota((FULL, capacity), 0))
    chosen = contract(by_holder, by_row, 1, 1).astype(bf16)
    ranks = contract(chosen, before, 1, 0)
    sizes = contract(chosen, jnp.ones((FULL, FULL), bf16), 1, 0)
    sizes_b = sizes.astype(bf16)
    from_s = iota((FULL, FULL), 1)
    to_s = iota((FULL, FULL), 0)
    ahead = marks((from_s // PAIR == to_s // PAIR) & (from_s < to_s))
    offsets = contract(ahead, sizes_b, 1, 0)
    offs[...] = offsets
    lens[...] = sizes
    group_lane = iota((planes, FULL), 1) // PAIR
    group_row = iota((planes, FULL), 0)
    grouped = marks(group_lane == group_row)
    amount = contract(grouped, sizes_b, 1, 0).astype(i32)
    so_far = contract(marks(group_lane <= group_row), sizes_b, 1, 0).astype(i32)
    live = so_far[planes - 1 : planes, :]
    excess = so_far - ((live * (group_row + 1)) >> 3)
    middle = (jnp.max(excess, axis=0, keepdims=True) + jnp.min(excess, axis=0, keepdims=True)) >> 1
    flow = excess - middle
    rising = jnp.maximum(flow, 0)
    sinking = jnp.maximum(-flow, 0)
    risen = previous(rising)
    keep = amount - rising - previous(sinking)
    up_at = following(keep)
    down_at = previous(keep + risen)
    for i, table in enumerate((keep, rising, risen, sinking)):
        tables[i] = table

    def spread(x):
        return contract(grouped, x.astype(bf16), 0, 0)

    keep_s, rising_s = spread(keep), spread(rising)
    dest = offsets + ranks - keep_s
    goes_up = (dest >= 0) & (dest < rising_s)
    goes_down = dest >= rising_s
    spot = jnp.where(
        dest < 0, dest + keep_s, jnp.where(goes_up, spread(up_at) + dest, spread(down_at) + dest - rising_s)
    )
    goes_down = (dest >= 0) & goes_down
    shift = jnp.where(goes_up, 1.0, jnp.where(goes_down, -1.0, 0.0))

    def per_slot(x):
        return jnp.sum(
            contract(x.astype(bf16), by_holder, 0, 0) * by_row.astype(f32), axis=0, keepdims=True
        ).astype(i32)

    slot = per_slot(spot)
    block = ((mine >> 11) + per_slot(shift)) & (planes - 1)
    when = jnp.where(slot < HALF, z - block, block - z) & (planes - 1)
    meta[0:1, :] = jnp.where(mine < 0, -1, when * CAP + slot)
    meta[1:2, :] = block
    meta[2:3, :] = jnp.where(mine < 0, -1, slot)

    own_group = pl.ds(pl.multiple_of(z * PAIR, PAIR), PAIR)
    widen = marks(iota((PAIR, pairs), 1) // PAIR == iota((PAIR, pairs), 0))
    start = contract(offs[own_group, :].astype(bf16), widen, 0, 0).astype(i32)
    size = contract(lens[own_group, :].astype(bf16), widen, 0, 0).astype(i32)
    index = iota((CAP, pairs), 1) & (PAIR - 1)
    spot_here = jnp.where(index < size, start + index, -1)

    def own(i):
        return tables[i, pl.ds(z, 1), :][:, 0:1]

    keep_z, rising_z, risen_z, sinking_z = own(0), own(1), own(2), own(3)
    line = iota((CAP, pairs), 0)
    pack_sel[:, 0:pairs] = marks((spot_here == line) & (line < keep_z))
    lane = iota((CAP, FULL), 1)
    line = iota((CAP, FULL), 0) - keep_z
    pack_sel[:, pairs : pairs + FULL] = marks(
        ((lane < SPILL) & (lane < risen_z) & (line == lane))
        | ((lane >= SPILL) & (lane < SPILL + sinking_z) & (line - risen_z == lane - SPILL))
    )
    line = iota((2 * SPILL, pairs), 0)
    above = spot_here[0 : 2 * SPILL, :] - keep_z
    spill_sel[...] = marks(
        ((line < SPILL) & (line < rising_z) & (above == line))
        | ((line >= SPILL) & (above - rising_z == line - SPILL) & (spot_here[0 : 2 * SPILL, :] >= 0))
    )

    all_codes = codes[...] >> 11
    held_by = [
        jnp.sum(jnp.where(all_codes == i, 1, 0), axis=1, keepdims=True) for i in range(planes)
    ]
    running = [held_by[0]]
    for i in range(1, planes):
        running.append(running[-1] + held_by[i])
    over = [running[i] - ((running[-1] * (i + 1)) >> 3) for i in range(planes)]
    most, least = over[0], over[0]
    for x in over[1:]:
        most, least = jnp.maximum(most, x), jnp.minimum(least, x)
    mid = (most + least) >> 1
    bad = jnp.maximum(most - mid, mid - least) - SPILL
    for i in range(planes):
        leaves = jnp.maximum(over[i] - mid, 0) + jnp.maximum(mid - over[i - 1], 0)
        bad = jnp.maximum(bad, leaves - held_by[i])
    misfit[0] = jnp.max(bad)

    for a in range(2):
        for j in range(2):
            came[a, j, pairs + 2 * SPILL :, :] = jnp.zeros((FULL - 2 * SPILL, piece), bf16)
    for a in range(2):
        for j in range(2):
            for k in range(1, experts):
                go_copy(a, j, k).wait()
            spilled[a, j] = contract(spill_sel[...], came[a, j, 0:pairs, :], 1, 0).astype(bf16)
            spill_up(a, j).start()
            spill_down(a, j).start()
            for p in range(2 * a + j):
                forward(p, 2 * a + j - p)
            spill_up(a, j).wait()
            spill_down(a, j).wait()
            allrows[a, 2 * c + j, 0] = contract(pack_sel[...], came[a, j], 1, 0).astype(bf16)
            ring_up(a, j, 0).start()
            ring_down(a, j, 0).start()
            twin_copy(a, j, 0).start()
    load_in.wait()
    load_out.wait()

    def step(t, carry):
        @pl.when(t > 0)
        def _():
            for p in range(3):
                forward(p, t + 3 - p)

        for j in range(2):
            twin_copy(0, j, t).wait_recv()
        pre = contract(allrows[0, 0, t], win[0], 1, 0)
        for q in range(1, PIECES):
            pre += contract(allrows[0, q, t], win[q], 1, 0)
        act, slope = gelu_parts(pre)
        gate = jnp.sum(
            jnp.where(meta[0:1, :] == iota((CAP, capacity), 0) + t * CAP, gates[...], 0.0),
            axis=1,
            keepdims=True,
        )
        act_s[t] = (gate * act).astype(bf16)

        @pl.when(t > 0)
        def _():
            forward(3, t)

        for j in range(2):
            twin_copy(1, j, t).wait_recv()
        back = contract(allrows[1, 0, t], wout[:, 0:piece], 1, 1)
        for q in range(1, PIECES):
            back += contract(allrows[1, q, t], wout[:, q * piece : (q + 1) * piece], 1, 1)
        back_pre = (gate * back * slope).astype(bf16)
        back_s[t] = back_pre
        gate_row = row_sums(act * back)
        gate_lo[pl.ds(lax.rem(z + planes - t, planes), 1), :] = gate_row
        gate_hi[pl.ds(lax.rem(z + t, planes), 1), :] = gate_row

        for j in range(2):

            @pl.when(t > 1)
            def _():
                part_copy(j, t - 2).wait_send()

            part_out[lax.rem(t, 2), j] = contract(back_pre, win[2 * other + j], 1, 1).astype(bf16)
            part_copy(j, t).start()
        for j in range(2):
            own_part = contract(back_pre, win[2 * c + j], 1, 1)
            part_copy(j, t).wait_recv()
            own_part += part_in[t, j].astype(f32)

            @pl.when(t == 0)
            def _():
                home[j] = own_part

            @pl.when(t > 2)
            def _():
                sum_up(j, t - 2).wait_send()
                sum_down(j, t - 2).wait_send()

            @pl.when(t > 1)
            def _():
                sum_up(j, t - 1).wait_recv()
                sum_down(j, t - 1).wait_recv()
                sum_out[lax.rem(t, 2), j] = (own_part + sum_in[t - 1, j].astype(f32)).astype(bf16)

            @pl.when(t == 1)
            def _():
                sum_out[lax.rem(t, 2), j] = own_part.astype(bf16)

            @pl.when(t > 0)
            def _():
                sum_up(j, t).start()
                sum_down(j, t).start()

        return carry

    lax.fori_loop(0, planes, step, 0)

    gate_all[me] = jnp.where(iota(gate_lo.shape, 1) < HALF, gate_lo[...], gate_hi[...])

    def gate_copy(k):
        return remote(
            gate_all.at[me], gate_all.at[me], gate_send.at[k], gate_recv.at[k], column_peers[k - 1]
        )

    for k in range(1, 2 * planes):
        gate_copy(k).start()

    rows = planes * CAP
    act_all = act_s[...].reshape(rows, act_s.shape[2])
    for q in range(PIECES):
        d_out[q] = contract(act_all, allrows[1, q].reshape(rows, piece), 0, 0).astype(bf16)

    last = planes - 1
    for j in range(2):
        sum_up(j, last).wait_recv()
        sum_down(j, last).wait_recv()
        slot_grad = (home[j] + sum_in[last, j].astype(f32)).astype(bf16)
        grad_go[j, pairs:, :] = contract(pack_sel[:, pairs:], slot_grad, 0, 0).astype(bf16)
        ret_up(j).start()
        ret_down(j).start()
        grad_go[j, 0:pairs, :] = contract(pack_sel[:, 0:pairs], slot_grad, 0, 0).astype(bf16)
        ret_up(j).wait()
        ret_down(j).wait()
        returned = contract(spill_sel[...], grad_ret[j], 0, 0)
        grad_go[j, 0:pairs, :] = (grad_go[j, 0:pairs, :].astype(f32) + returned).astype(bf16)
        grad_came[j, own_rows, :] = grad_go[j, own_rows, :]
        for k in range(1, experts):
            grad_copy(j, k).start()

    stores = []
    for q in range(PIECES):
        cp = pltpu.make_async_copy(
            d_out.at[q], d_out_hbm.at[:, pl.ds(q * piece, piece)], store_sem.at[q]
        )
        cp.start()
        stores.append(cp)
    back_all = back_s[...].reshape(rows, back_s.shape[2])
    for q in range(PIECES):
        turned = contract(back_all, allrows[0, q].reshape(rows, piece), 0, 0)
        d_in[q] = turned.T.astype(bf16)
        cp = pltpu.make_async_copy(d_in.at[q], d_in_hbm.at[q], store_sem.at[PIECES + q])
        cp.start()
        stores.append(cp)

    for k in range(1, 2 * planes):
        gate_copy(k).wait()
    total = gate_all[0]
    for i in range(1, 2 * planes):
        total += gate_all[i]
    own_lanes = pl.ds(pl.multiple_of(z * CAP, CAP), CAP)
    found = marks(meta[2:3, own_lanes] == iota((CAP, CAP), 0))
    values = sum(contract(part, found, 1, 0) for part in split_three(total))
    values = jnp.sum(
        jnp.where(meta[1:2, own_lanes] == iota(values.shape, 0), values, 0.0),
        axis=0,
        keepdims=True,
    )
    d_gates[...] = jnp.where(c == 0, values[:, 0:HALF], values[:, HALF:])

    for j in range(2):
        for k in range(1, experts):
            grad_copy(j, k).wait()
        d_tok[j] = contract(pick_sel[...], grad_came[j], 0, 0).astype(bf16)
        cp = pltpu.make_async_copy(
            d_tok.at[j], d_tok_hbm.at[:, pl.ds(j * piece, piece)], store_sem.at[2 * PIECES + j]
        )
        cp.start()
        stores.append(cp)

    for a in range(2):
        for j in range(2):
            for t in range(planes):
                twin_copy(a, j, t).wait_send()
                if t < planes - 1:
                    ring_up(a, j, t).wait_send()
                    ring_down(a, j, t).wait_send()
    for j in range(2):
        for t in (planes - 2, planes - 1):
            part_copy(j, t).wait_send()
            sum_up(j, t).wait_send()
            sum_down(j, t).wait_send()
    for cp in stores:
        cp.wait()


def fast(tokens, cotangent, w_in, w_out, gates, picks, counts):
    planes = lax.axis_size("patch")
    experts = lax.axis_size("expert")
    tok_dev, width = tokens.shape
    units = w_in.shape[2]
    capacity = picks.shape[1]
    piece = width // PIECES
    pairs = experts * PAIR
    vmem = pl.BlockSpec(memory_space=pltpu.VMEM)
    smem = pl.BlockSpec(memory_space=pltpu.SMEM)
    hbm = pl.BlockSpec(memory_space=pl.ANY)
    dma = pltpu.SemaphoreType.DMA
    scratch = [
        pltpu.VMEM((experts, capacity), i32),
        pltpu.VMEM((experts, tok_dev), f32),
        pltpu.VMEM((8, capacity), i32),
        pltpu.VMEM((4, planes, FULL), i32),
        pltpu.VMEM((FULL, FULL), f32),
        pltpu.VMEM((FULL, FULL), f32),
        pltpu.VMEM((pairs, tok_dev), bf16),
        pltpu.VMEM((CAP, pairs + FULL), bf16),
        pltpu.VMEM((2 * SPILL, pairs), bf16),
        pltpu.VMEM((2, 2, tok_dev, piece), bf16),
        pltpu.VMEM((2, 2, pairs, piece), bf16),
        pltpu.VMEM((2, 2, pairs + FULL, piece), bf16),
        pltpu.VMEM((2, 2, 2 * SPILL, piece), bf16),
        pltpu.VMEM((2, PIECES, planes, CAP, piece), bf16),
        pltpu.VMEM((PIECES, piece, units), bf16),
        pltpu.VMEM((units, width), bf16),
        pltpu.VMEM((planes, CAP, units), bf16),
        pltpu.VMEM((planes, CAP, units), bf16),
        pltpu.VMEM((2, CAP, piece), f32),
        pltpu.VMEM((2, 2, CAP, piece), bf16),
        pltpu.VMEM((planes, 2, CAP, piece), bf16),
        pltpu.VMEM((2, 2, CAP, piece), bf16),
        pltpu.VMEM((planes, 2, CAP, piece), bf16),
        pltpu.VMEM((2, pairs + FULL, piece), bf16),
        pltpu.VMEM((2, pairs, piece), bf16),
        pltpu.VMEM((2, 2 * SPILL, piece), bf16),
        pltpu.VMEM((2, tok_dev, piece), bf16),
        pltpu.VMEM((PIECES, piece, units), bf16),
        pltpu.VMEM((PIECES, units, piece), bf16),
        pltpu.VMEM((planes, CAP), f32),
        pltpu.VMEM((planes, CAP), f32),
        pltpu.VMEM((2 * planes, planes, CAP), f32),
        dma((6,)),
        dma((2, 2, experts)),
        dma((2, 2, experts)),
        dma((2, 2, 2)),
        dma((2, 2, 2)),
        dma((2, 2, 2, planes)),
        dma((2, 2, 2, planes)),
        dma((2, 2, planes)),
        dma((2, 2, planes)),
        dma((planes, 2)),
        dma((planes, 2)),
        dma((2, 2, planes)),
        dma((2, 2, planes)),
        dma((2, 2)),
        dma((2, 2)),
        dma((2, experts)),
        dma((2, experts)),
        dma((2 * planes,)),
        dma((2 * planes,)),
        dma((2 * PIECES + 2,)),
    ]
    d_tokens, d_in, d_out, d_gates, misfit = pl.pallas_call(
        functools.partial(kernel, planes, experts),
        out_shape=(
            jax.ShapeDtypeStruct((tok_dev, width // 2), bf16),
            jax.ShapeDtypeStruct((PIECES, piece, units), bf16),
            jax.ShapeDtypeStruct((units, width), bf16),
            jax.ShapeDtypeStruct((1, HALF), f32),
            jax.ShapeDtypeStruct((1,), i32),
        ),
        in_specs=[hbm, hbm, hbm, hbm, vmem, vmem, smem],
        out_specs=(hbm, hbm, hbm, vmem, smem),
        scratch_shapes=scratch,
        compiler_params=pltpu.CompilerParams(
            collective_id=0, has_side_effects=True, vmem_limit_bytes=60 * 2**20
        ),
    )(tokens, cotangent, w_in.reshape(PIECES, piece, units), w_out[0], gates, picks, counts)
    return (d_tokens, d_in.reshape(w_in.shape), d_out[None], d_gates, misfit)


def local(*args):
    results = fast(*args)
    return lax.cond(
        results[4][0] <= 0, lambda found, args: found, lambda found, args: general(*args), results[:4], args
    )


def solution(mesh):
    in_specs = (
        P(("patch", "expert"), None),
        P(("patch", "expert"), None),
        P("expert", None, ("patch", "hidden")),
        P("expert", ("patch", "hidden"), None),
        P("expert", None),
        P(),
        P(),
    )
    out_specs = (
        P(("patch", "expert"), "hidden"),
        P("expert", None, ("patch", "hidden")),
        P("expert", ("patch", "hidden"), None),
        P("expert", ("patch", "hidden")),
    )
    return jax.shard_map(local, mesh=mesh, in_specs=in_specs, out_specs=out_specs, check_vma=False)
```

```python
import functools

import jax
import jax.numpy as jnp
from jax import lax
from jax.experimental import pallas as pl
from jax.experimental.pallas import tpu as pltpu
from jax.sharding import PartitionSpec as P

inv_root_two = 0.7071067811865476
inv_root_two_pi = 0.3989422804014327


def gelu_parts(pre):
    normal_cdf = 0.5 * (1.0 + lax.erf(pre * inv_root_two))
    density = jnp.exp(-0.5 * pre * pre) * inv_root_two_pi
    return (pre * normal_cdf, normal_cdf + pre * density)


MESH = pl.DeviceIdType.MESH
f32 = jnp.float32
bf16 = jnp.bfloat16
i32 = jnp.int32
PAIR = 16
PIECES = 4
OWN = PIECES // 2
STRIDE = max(1, PIECES // 4)
SUMS = 2
CAP = 128
HALF = CAP // 2
SPILL = 32
FULL = 128


def contract(a, b, dim_a, dim_b):
    return lax.dot_general(a, b, (((dim_a,), (dim_b,)), ((), ())), preferred_element_type=f32)


def marks(mask):
    return jnp.where(mask, 1.0, 0.0).astype(bf16)


def iota(shape, dim):
    return lax.broadcasted_iota(i32, shape, dim)


def split_three(x):
    a = x.astype(bf16)
    rest = x - a.astype(f32)
    b = rest.astype(bf16)
    return (a, b, (rest - b.astype(f32)).astype(bf16))


def row_sums(x):
    ones = jnp.ones((8, x.shape[1]), bf16)
    return sum(contract(ones, part, 1, 1) for part in split_three(x))[0:1]


def previous(x):
    return pltpu.roll(x, 1, 0)


def following(x):
    return pltpu.roll(x, x.shape[0] - 1, 0)


def kernel(
    planes,
    experts,
    tokens,
    cotangent,
    w_in_hbm,
    w_out_hbm,
    gates,
    picks,
    counts,
    window,
    d_tok_hbm,
    d_in_hbm,
    d_out_hbm,
    d_gates,
    misfit,
    codes,
    taken,
    meta,
    tables,
    offs,
    lens,
    pick_sel,
    pack_sel,
    spill_sel,
    held,
    going,
    came,
    spilled,
    allrows,
    win,
    wout,
    act_s,
    back_s,
    home,
    part_out,
    part_in,
    sum_out,
    sum_in,
    grad_go,
    grad_came,
    grad_ret,
    d_tok,
    d_in,
    d_out,
    gate_lo,
    gate_hi,
    gate_all,
    load_sem,
    go_send,
    go_recv,
    spill_send,
    spill_recv,
    ring_send,
    ring_recv,
    twin_send,
    twin_recv,
    part_send,
    part_recv,
    sum_send,
    sum_recv,
    ret_send,
    ret_recv,
    grad_send,
    grad_recv,
    gate_send,
    gate_recv,
    store_sem,
):
    z = lax.axis_index("patch")
    e = lax.axis_index("expert")
    c = lax.axis_index("hidden")
    other = 1 - c
    up = (lax.rem(z + 1, planes), e, c)
    down = (lax.rem(z + planes - 1, planes), e, c)
    twin = (z, e, other)
    piece = held.shape[3]
    pairs = experts * PAIR
    capacity = codes.shape[1]
    plane_peers = [(z, lax.rem(e + k, experts), c) for k in range(1, experts)]
    me = z * 2 + c
    column_ids = [lax.rem(me + k, 2 * planes) for k in range(1, 2 * planes)]
    column_peers = [(i // 2, e, lax.rem(i, 2)) for i in column_ids]

    barrier = pltpu.get_barrier_semaphore()
    for peer in plane_peers + column_peers:
        pl.semaphore_signal(barrier, inc=1, device_id=peer, device_id_type=MESH)

    loads = []
    for a, ref in enumerate((tokens, cotangent)):
        for j in range(OWN):
            col = pl.multiple_of((OWN * c + j) * piece, piece)
            cp = pltpu.make_async_copy(
                ref.at[:, pl.ds(col, piece)], held.at[a, j], load_sem.at[OWN * a + j]
            )
            cp.start()
            loads.append(cp)
    load_in = pltpu.make_async_copy(w_in_hbm, win, load_sem.at[PIECES])
    load_out = pltpu.make_async_copy(w_out_hbm, wout, load_sem.at[PIECES + 1])
    load_in.start()
    load_out.start()

    before = marks(iota((FULL, FULL), 0) < iota((FULL, FULL), 1))
    place = iota((1, capacity), 1)
    for i in range(experts):
        codes[i : i + 1, :] = jnp.where(place < counts[i], picks[i : i + 1, :], -1)
    base = (z * experts + e) * FULL
    wanted = iota((FULL, capacity), 0) + base

    def find(i, carry):
        match = jnp.where(codes[pl.ds(i, 1), :] == wanted, 1.0, 0.0)
        folded = match[:, 0:FULL]
        for k in range(1, capacity // FULL):
            folded += match[:, k * FULL : (k + 1) * FULL]
        taken[pl.ds(i, 1), :] = contract(jnp.ones((8, FULL), bf16), folded.astype(bf16), 1, 1)[0:1]
        return carry

    lax.fori_loop(0, experts, find, 0, unroll=4)
    present = taken[...]
    order = contract(present.astype(bf16), before, 1, 0)
    order = jnp.where(present > 0.5, order, -1.0).astype(i32)
    for i in range(experts):
        pick_sel[i * PAIR : (i + 1) * PAIR, :] = marks(
            iota((PAIR, FULL), 0) == order[i : i + 1, :]
        )

    pl.semaphore_wait(barrier, len(plane_peers) + len(column_peers))

    def remote(src, dst, s, r, dev):
        return pltpu.make_async_remote_copy(
            src_ref=src, dst_ref=dst, send_sem=s, recv_sem=r, device_id=dev, device_id_type=MESH
        )

    own_rows = pl.ds(pl.multiple_of(e * PAIR, PAIR), PAIR)

    def plane_copy(src, dst, ssem, rsem, k):
        to = pl.multiple_of(lax.rem(e + k, experts) * PAIR, PAIR)
        return remote(
            src.at[pl.ds(to, PAIR)], dst.at[own_rows], ssem.at[k], rsem.at[k], plane_peers[k - 1]
        )

    def go_copy(a, j, k):
        return plane_copy(
            going.at[a, j], came.at[a, j], go_send.at[a, j], go_recv.at[a, j], k
        )

    def grad_copy(j, k):
        return plane_copy(
            grad_go.at[j], grad_came.at[j], grad_send.at[j], grad_recv.at[j], k
        )

    def spill_up(a, j):
        return remote(
            spilled.at[a, j, pl.ds(0, SPILL)],
            came.at[a, j, pl.ds(pairs, SPILL)],
            spill_send.at[0, a, j],
            spill_recv.at[0, a, j],
            up,
        )

    def spill_down(a, j):
        return remote(
            spilled.at[a, j, pl.ds(SPILL, SPILL)],
            came.at[a, j, pl.ds(pairs + SPILL, SPILL)],
            spill_send.at[1, a, j],
            spill_recv.at[1, a, j],
            down,
        )

    def ret_down(j):
        return remote(
            grad_go.at[j, pl.ds(pairs, SPILL)],
            grad_ret.at[j, pl.ds(0, SPILL)],
            ret_send.at[0, j],
            ret_recv.at[0, j],
            down,
        )

    def ret_up(j):
        return remote(
            grad_go.at[j, pl.ds(pairs + SPILL, SPILL)],
            grad_ret.at[j, pl.ds(SPILL, SPILL)],
            ret_send.at[1, j],
            ret_recv.at[1, j],
            up,
        )

    def ring_up(a, j, t):
        q = OWN * c + j
        return remote(
            allrows.at[a, q, t, pl.ds(0, HALF)],
            allrows.at[a, q, t + 1, pl.ds(0, HALF)],
            ring_send.at[0, a, j, t],
            ring_recv.at[0, a, j, t + 1],
            up,
        )

    def ring_down(a, j, t):
        q = OWN * c + j
        return remote(
            allrows.at[a, q, t, pl.ds(HALF, HALF)],
            allrows.at[a, q, t + 1, pl.ds(HALF, HALF)],
            ring_send.at[1, a, j, t],
            ring_recv.at[1, a, j, t + 1],
            down,
        )

    def twin_copy(a, j, t):
        q = OWN * c + j
        return remote(
            allrows.at[a, q, t],
            allrows.at[a, q, t],
            twin_send.at[a, j, t],
            twin_recv.at[a, j, t],
            twin,
        )

    def part_copy(j, t):
        slot = lax.rem(t, 2)
        return remote(
            part_out.at[slot, j], part_in.at[t, j], part_send.at[t, j], part_recv.at[t, j], twin
        )

    def sum_up(j, t):
        return remote(
            sum_out.at[lax.rem(t, 2), j, pl.ds(0, HALF)],
            sum_in.at[t, j, pl.ds(0, HALF)],
            sum_send.at[0, j, t],
            sum_recv.at[0, j, t],
            up,
        )

    def sum_down(j, t):
        return remote(
            sum_out.at[lax.rem(t, 2), j, pl.ds(HALF, HALF)],
            sum_in.at[t, j, pl.ds(HALF, HALF)],
            sum_send.at[1, j, t],
            sum_recv.at[1, j, t],
            down,
        )

    for a in range(2):
        for j in range(OWN):
            loads[OWN * a + j].wait()
            going[a, j] = contract(pick_sel[...], held[a, j], 1, 0).astype(bf16)
            came[a, j, own_rows, :] = going[a, j, own_rows, :]
            for k in range(1, experts):
                go_copy(a, j, k).start()

    def forward(p, t):
        a, j = p // OWN, p % OWN

        @pl.when(t < planes)
        def _():
            ring_up(a, j, t - 1).wait_recv()

            @pl.when(t < planes - 1)
            def _():
                ring_up(a, j, t).start()

            ring_down(a, j, t - 1).wait_recv()

            @pl.when(t < planes - 1)
            def _():
                ring_down(a, j, t).start()

            twin_copy(a, j, t).start()

    mine = codes[pl.ds(e, 1), :]
    by_holder = marks((mine >> 7) == iota((FULL, capacity), 0))
    by_row = marks((mine & (FULL - 1)) == iota((FULL, capacity), 0))
    chosen = contract(by_holder, by_row, 1, 1).astype(bf16)
    ranks = contract(chosen, before, 1, 0)
    sizes = contract(chosen, jnp.ones((FULL, FULL), bf16), 1, 0)
    sizes_b = sizes.astype(bf16)
    from_s = iota((FULL, FULL), 1)
    to_s = iota((FULL, FULL), 0)
    ahead = marks((from_s // PAIR == to_s // PAIR) & (from_s < to_s))
    offsets = contract(ahead, sizes_b, 1, 0)
    offs[...] = offsets
    lens[...] = sizes
    group_lane = iota((planes, FULL), 1) // PAIR
    group_row = iota((planes, FULL), 0)
    grouped = marks(group_lane == group_row)
    amount = contract(grouped, sizes_b, 1, 0).astype(i32)
    so_far = contract(marks(group_lane <= group_row), sizes_b, 1, 0).astype(i32)
    live = so_far[planes - 1 : planes, :]
    excess = so_far - ((live * (group_row + 1)) >> 3)
    middle = (jnp.max(excess, axis=0, keepdims=True) + jnp.min(excess, axis=0, keepdims=True)) >> 1
    balanced = window[0] == 0
    begin = jnp.maximum(window[0] - 1, 0) * CAP
    flow = jnp.where(balanced, excess - middle, 0)
    rising = jnp.maximum(flow, 0)
    sinking = jnp.maximum(-flow, 0)
    risen = previous(rising)
    keep = amount - rising - previous(sinking)
    keep = jnp.where(balanced, keep, jnp.clip(amount - begin, 0, CAP))
    up_at = following(keep)
    down_at = previous(keep + risen)
    for i, table in enumerate((keep, rising, risen, sinking)):
        tables[i] = table

    def spread(x):
        return contract(grouped, x.astype(bf16), 0, 0)

    keep_s, rising_s = spread(keep), spread(rising)
    dest = offsets + ranks - begin.astype(f32)
    held_here = balanced | ((dest >= 0) & (dest < keep_s))
    dest -= keep_s
    goes_up = (dest >= 0) & (dest < rising_s)
    goes_down = dest >= rising_s
    spot = jnp.where(
        dest < 0, dest + keep_s, jnp.where(goes_up, spread(up_at) + dest, spread(down_at) + dest - rising_s)
    )
    spot = jnp.where(held_here, spot, -1.0)
    goes_down = (dest >= 0) & goes_down
    shift = jnp.where(goes_up, 1.0, jnp.where(goes_down, -1.0, 0.0))

    def per_slot(x):
        return jnp.sum(
            contract(x.astype(bf16), by_holder, 0, 0) * by_row.astype(f32), axis=0, keepdims=True
        ).astype(i32)

    slot = per_slot(spot)
    block = ((mine >> 11) + per_slot(shift)) & (planes - 1)
    when = jnp.where(slot < HALF, z - block, block - z) & (planes - 1)
    unused = (mine < 0) | (slot < 0)
    meta[0:1, :] = jnp.where(unused, -1, when * CAP + slot)
    meta[1:2, :] = block
    meta[2:3, :] = jnp.where(unused, -1, slot)

    own_group = pl.ds(pl.multiple_of(z * PAIR, PAIR), PAIR)
    widen = marks(iota((PAIR, pairs), 1) // PAIR == iota((PAIR, pairs), 0))
    start = contract(offs[own_group, :].astype(bf16), widen, 0, 0).astype(i32)
    size = contract(lens[own_group, :].astype(bf16), widen, 0, 0).astype(i32)
    index = iota((CAP, pairs), 1) & (PAIR - 1)
    spot_here = jnp.where(index < size, jnp.maximum(start + index - begin, -1), -1)

    def own(i):
        return tables[i, pl.ds(z, 1), :][:, 0:1]

    keep_z, rising_z, risen_z, sinking_z = own(0), own(1), own(2), own(3)
    line = iota((CAP, pairs), 0)
    pack_sel[:, 0:pairs] = marks((spot_here == line) & (line < keep_z))
    lane = iota((CAP, FULL), 1)
    line = iota((CAP, FULL), 0) - keep_z
    pack_sel[:, pairs : pairs + FULL] = marks(
        ((lane < SPILL) & (lane < risen_z) & (line == lane))
        | ((lane >= SPILL) & (lane < SPILL + sinking_z) & (line - risen_z == lane - SPILL))
    )
    line = iota((2 * SPILL, pairs), 0)
    above = spot_here[0 : 2 * SPILL, :] - keep_z
    spill_sel[...] = marks(
        ((line < SPILL) & (line < rising_z) & (above == line))
        | ((line >= SPILL) & (above - rising_z == line - SPILL) & (spot_here[0 : 2 * SPILL, :] >= 0))
    )

    all_codes = codes[...] >> 11
    held_by = [
        jnp.sum(jnp.where(all_codes == i, 1, 0), axis=1, keepdims=True) for i in range(planes)
    ]
    running = [held_by[0]]
    for i in range(1, planes):
        running.append(running[-1] + held_by[i])
    over = [running[i] - ((running[-1] * (i + 1)) >> 3) for i in range(planes)]
    most, least = over[0], over[0]
    for x in over[1:]:
        most, least = jnp.maximum(most, x), jnp.minimum(least, x)
    mid = (most + least) >> 1
    bad = jnp.maximum(most - mid, mid - least) - SPILL
    for i in range(planes):
        leaves = jnp.maximum(over[i] - mid, 0) + jnp.maximum(mid - over[i - 1], 0)
        bad = jnp.maximum(bad, leaves - held_by[i])
    misfit[0] = jnp.max(bad)

    for a in range(2):
        for j in range(OWN):
            came[a, j, pairs + 2 * SPILL :, :] = jnp.zeros((FULL - 2 * SPILL, piece), bf16)
    for a in range(2):
        for j in range(OWN):
            for k in range(1, experts):
                go_copy(a, j, k).wait()
            spilled[a, j] = contract(spill_sel[...], came[a, j, 0:pairs, :], 1, 0).astype(bf16)
            spill_up(a, j).start()
            spill_down(a, j).start()
            for p in range((OWN * a + j) % STRIDE, OWN * a + j, STRIDE):
                forward(p, (OWN * a + j - p) // STRIDE)
            spill_up(a, j).wait()
            spill_down(a, j).wait()
            allrows[a, OWN * c + j, 0] = contract(pack_sel[...], came[a, j], 1, 0).astype(bf16)
            ring_up(a, j, 0).start()
            ring_down(a, j, 0).start()
            twin_copy(a, j, 0).start()
    load_in.wait()
    load_out.wait()

    narrow = home.shape[2]

    def weights(core, j):
        begin = j * narrow
        return win[OWN * core + begin // piece, begin % piece : begin % piece + narrow]

    def step(t, carry):
        for j in range(OWN):
            twin_copy(0, j, t).wait_recv()
        pre = contract(allrows[0, 0, t], win[0], 1, 0)
        for q in range(1, PIECES):
            pre += contract(allrows[0, q, t], win[q], 1, 0)
        act, slope = gelu_parts(pre)
        gate = jnp.sum(
            jnp.where(meta[0:1, :] == iota((CAP, capacity), 0) + t * CAP, gates[...], 0.0),
            axis=1,
            keepdims=True,
        )
        act_s[t] = (gate * act).astype(bf16)

        @pl.when(t > 0)
        def _():
            for p in range(PIECES - STRIDE, PIECES):
                forward(p, t)

        for j in range(OWN):
            twin_copy(1, j, t).wait_recv()
        back = contract(allrows[1, 0, t], wout[:, 0:piece], 1, 1)
        for q in range(1, PIECES):
            back += contract(allrows[1, q, t], wout[:, q * piece : (q + 1) * piece], 1, 1)
        back_pre = (gate * back * slope).astype(bf16)
        back_s[t] = back_pre
        gate_row = row_sums(act * back)
        gate_lo[pl.ds(lax.rem(z + planes - t, planes), 1), :] = gate_row
        gate_hi[pl.ds(lax.rem(z + t, planes), 1), :] = gate_row

        for j in range(SUMS):

            @pl.when(t > 1)
            def _():
                part_copy(j, t - 2).wait_send()

            part_out[lax.rem(t, 2), j] = contract(back_pre, weights(other, j), 1, 1).astype(bf16)
            part_copy(j, t).start()
        for p in range(PIECES - STRIDE):
            forward(p, t + 1 + (PIECES - 1 - p) // STRIDE)
        for j in range(SUMS):
            own_part = contract(back_pre, weights(c, j), 1, 1)
            part_copy(j, t).wait_recv()
            own_part += part_in[t, j].astype(f32)

            @pl.when(t == 0)
            def _():
                home[j] = own_part

            @pl.when(t > 2)
            def _():
                sum_up(j, t - 2).wait_send()
                sum_down(j, t - 2).wait_send()

            @pl.when(t > 1)
            def _():
                sum_up(j, t - 1).wait_recv()
                sum_down(j, t - 1).wait_recv()
                sum_out[lax.rem(t, 2), j] = (own_part + sum_in[t - 1, j].astype(f32)).astype(bf16)

            @pl.when(t == 1)
            def _():
                sum_out[lax.rem(t, 2), j] = own_part.astype(bf16)

            @pl.when(t > 0)
            def _():
                sum_up(j, t).start()
                sum_down(j, t).start()

        return carry

    lax.fori_loop(0, planes, step, 0)

    gate_all[me] = jnp.where(iota(gate_lo.shape, 1) < HALF, gate_lo[...], gate_hi[...])

    def gate_copy(k):
        return remote(
            gate_all.at[me], gate_all.at[me], gate_send.at[k], gate_recv.at[k], column_peers[k - 1]
        )

    for k in range(1, 2 * planes):
        gate_copy(k).start()

    rows = planes * CAP
    act_all = act_s[...].reshape(rows, act_s.shape[2])
    for q in range(PIECES):
        d_out[q] = contract(act_all, allrows[1, q].reshape(rows, piece), 0, 0).astype(bf16)

    last = planes - 1
    for j in range(SUMS):
        sum_up(j, last).wait_recv()
        sum_down(j, last).wait_recv()
        slot_grad = (home[j] + sum_in[last, j].astype(f32)).astype(bf16)
        grad_go[j, pairs:, :] = contract(pack_sel[:, pairs:], slot_grad, 0, 0).astype(bf16)
        ret_up(j).start()
        ret_down(j).start()
        grad_go[j, 0:pairs, :] = contract(pack_sel[:, 0:pairs], slot_grad, 0, 0).astype(bf16)
        ret_up(j).wait()
        ret_down(j).wait()
        returned = contract(spill_sel[...], grad_ret[j], 0, 0)
        grad_go[j, 0:pairs, :] = (grad_go[j, 0:pairs, :].astype(f32) + returned).astype(bf16)
        grad_came[j, own_rows, :] = grad_go[j, own_rows, :]
        for k in range(1, experts):
            grad_copy(j, k).start()

    stores = []
    for q in range(PIECES):
        cp = pltpu.make_async_copy(
            d_out.at[q], d_out_hbm.at[:, pl.ds(q * piece, piece)], store_sem.at[q]
        )
        cp.start()
        stores.append(cp)
    back_all = back_s[...].reshape(rows, back_s.shape[2])
    for q in range(PIECES):
        turned = contract(back_all, allrows[0, q].reshape(rows, piece), 0, 0)
        d_in[q] = turned.T.astype(bf16)
        cp = pltpu.make_async_copy(d_in.at[q], d_in_hbm.at[q], store_sem.at[PIECES + q])
        cp.start()
        stores.append(cp)

    for k in range(1, 2 * planes):
        gate_copy(k).wait()
    total = gate_all[0]
    for i in range(1, 2 * planes):
        total += gate_all[i]
    own_lanes = pl.ds(pl.multiple_of(z * CAP, CAP), CAP)
    found = marks(meta[2:3, own_lanes] == iota((CAP, CAP), 0))
    values = sum(contract(part, found, 1, 0) for part in split_three(total))
    values = jnp.sum(
        jnp.where(meta[1:2, own_lanes] == iota(values.shape, 0), values, 0.0),
        axis=0,
        keepdims=True,
    )
    d_gates[...] = jnp.where(c == 0, values[:, 0:HALF], values[:, HALF:])

    for j in range(SUMS):
        for k in range(1, experts):
            grad_copy(j, k).wait()
        d_tok[j] = contract(pick_sel[...], grad_came[j], 0, 0).astype(bf16)
        cp = pltpu.make_async_copy(
            d_tok.at[j], d_tok_hbm.at[:, pl.ds(j * narrow, narrow)], store_sem.at[2 * PIECES + j]
        )
        cp.start()
        stores.append(cp)

    for a in range(2):
        for j in range(OWN):
            for t in range(planes):
                twin_copy(a, j, t).wait_send()
                if t < planes - 1:
                    ring_up(a, j, t).wait_send()
                    ring_down(a, j, t).wait_send()
    for j in range(SUMS):
        for t in (planes - 2, planes - 1):
            part_copy(j, t).wait_send()
            sum_up(j, t).wait_send()
            sum_down(j, t).wait_send()
    for cp in stores:
        cp.wait()


def layer(window, tokens, cotangent, w_in, w_out, gates, picks, counts):
    planes = lax.axis_size("patch")
    experts = lax.axis_size("expert")
    tok_dev, width = tokens.shape
    units = w_in.shape[2]
    capacity = picks.shape[1]
    piece = width // PIECES
    narrow = width // 2 // SUMS
    pairs = experts * PAIR
    vmem = pl.BlockSpec(memory_space=pltpu.VMEM)
    smem = pl.BlockSpec(memory_space=pltpu.SMEM)
    hbm = pl.BlockSpec(memory_space=pl.ANY)
    dma = pltpu.SemaphoreType.DMA
    scratch = [
        pltpu.VMEM((experts, capacity), i32),
        pltpu.VMEM((experts, tok_dev), f32),
        pltpu.VMEM((8, capacity), i32),
        pltpu.VMEM((4, planes, FULL), i32),
        pltpu.VMEM((FULL, FULL), f32),
        pltpu.VMEM((FULL, FULL), f32),
        pltpu.VMEM((pairs, tok_dev), bf16),
        pltpu.VMEM((CAP, pairs + FULL), bf16),
        pltpu.VMEM((2 * SPILL, pairs), bf16),
        pltpu.VMEM((2, OWN, tok_dev, piece), bf16),
        pltpu.VMEM((2, OWN, pairs, piece), bf16),
        pltpu.VMEM((2, OWN, pairs + FULL, piece), bf16),
        pltpu.VMEM((2, OWN, 2 * SPILL, piece), bf16),
        pltpu.VMEM((2, PIECES, planes, CAP, piece), bf16),
        pltpu.VMEM((PIECES, piece, units), bf16),
        pltpu.VMEM((units, width), bf16),
        pltpu.VMEM((planes, CAP, units), bf16),
        pltpu.VMEM((planes, CAP, units), bf16),
        pltpu.VMEM((SUMS, CAP, narrow), f32),
        pltpu.VMEM((2, SUMS, CAP, narrow), bf16),
        pltpu.VMEM((planes, SUMS, CAP, narrow), bf16),
        pltpu.VMEM((2, SUMS, CAP, narrow), bf16),
        pltpu.VMEM((planes, SUMS, CAP, narrow), bf16),
        pltpu.VMEM((SUMS, pairs + FULL, narrow), bf16),
        pltpu.VMEM((SUMS, pairs, narrow), bf16),
        pltpu.VMEM((SUMS, 2 * SPILL, narrow), bf16),
        pltpu.VMEM((SUMS, tok_dev, narrow), bf16),
        pltpu.VMEM((PIECES, piece, units), bf16),
        pltpu.VMEM((PIECES, units, piece), bf16),
        pltpu.VMEM((planes, CAP), f32),
        pltpu.VMEM((planes, CAP), f32),
        pltpu.VMEM((2 * planes, planes, CAP), f32),
        dma((PIECES + 2,)),
        dma((2, OWN, experts)),
        dma((2, OWN, experts)),
        dma((2, 2, OWN)),
        dma((2, 2, OWN)),
        dma((2, 2, OWN, planes)),
        dma((2, 2, OWN, planes)),
        dma((2, OWN, planes)),
        dma((2, OWN, planes)),
        dma((planes, SUMS)),
        dma((planes, SUMS)),
        dma((2, SUMS, planes)),
        dma((2, SUMS, planes)),
        dma((2, SUMS)),
        dma((2, SUMS)),
        dma((SUMS, experts)),
        dma((SUMS, experts)),
        dma((2 * planes,)),
        dma((2 * planes,)),
        dma((2 * PIECES + SUMS,)),
    ]
    d_tokens, d_in, d_out, d_gates, misfit = pl.pallas_call(
        functools.partial(kernel, planes, experts),
        out_shape=(
            jax.ShapeDtypeStruct((tok_dev, width // 2), bf16),
            jax.ShapeDtypeStruct((PIECES, piece, units), bf16),
            jax.ShapeDtypeStruct((units, width), bf16),
            jax.ShapeDtypeStruct((1, HALF), f32),
            jax.ShapeDtypeStruct((1,), i32),
        ),
        in_specs=[hbm, hbm, hbm, hbm, vmem, vmem, smem, smem],
        out_specs=(hbm, hbm, hbm, vmem, smem),
        scratch_shapes=scratch,
        compiler_params=pltpu.CompilerParams(
            collective_id=0, has_side_effects=True, vmem_limit_bytes=60 * 2**20
        ),
    )(
        tokens,
        cotangent,
        w_in.reshape(PIECES, piece, units),
        w_out[0],
        gates,
        picks,
        counts,
        jnp.reshape(window, (1,)).astype(i32),
    )
    return (d_tokens, d_in.reshape(w_in.shape), d_out[None], d_gates, misfit)


def store(*refs):
    count = (len(refs) - 2) // 3
    came_sem, went_sem = refs[-2:]
    arriving, leaving = [], []
    for src, dst, mid in zip(refs[:count], refs[count : 2 * count], refs[2 * count :]):
        parts = 4 if src.shape[-2] > FULL else 1
        rows = src.shape[-2] // parts
        for i in range(parts):
            at = pl.ds(i * rows, rows)
            cut = (slice(None), at) if len(src.shape) > 2 else (at,)
            n = len(arriving)
            arriving.append(pltpu.make_async_copy(src.at[cut], mid.at[cut], came_sem.at[n]))
            leaving.append(pltpu.make_async_copy(mid.at[cut], dst.at[cut], went_sem.at[n]))
    for cp in arriving:
        cp.start()
    for first, second in zip(arriving, leaving):
        first.wait()
        second.start()
    for cp in leaving:
        cp.wait()


def local(*args):
    results = layer(0, *args)

    def windows(found, args):
        def add(i, total):
            part = layer(i + 1, *args)[:4]
            return tuple((x.astype(f32) + y.astype(f32)).astype(x.dtype) for x, y in zip(total, part))

        return lax.fori_loop(0, 2, add, tuple(jnp.zeros_like(x) for x in found))

    results = lax.cond(results[4][0] <= 0, lambda found, args: found, windows, results[:4], args)
    hbm = pl.BlockSpec(memory_space=pl.ANY)
    return pl.pallas_call(
        store,
        out_shape=tuple(jax.ShapeDtypeStruct(x.shape, x.dtype) for x in results),
        in_specs=[hbm] * 4,
        out_specs=(hbm,) * 4,
        scratch_shapes=[pltpu.VMEM(x.shape, x.dtype) for x in results]
        + [pltpu.SemaphoreType.DMA((12,))] * 2,
    )(*results)


def solution(mesh):
    in_specs = (
        P(("patch", "expert"), None),
        P(("patch", "expert"), None),
        P("expert", None, ("patch", "hidden")),
        P("expert", ("patch", "hidden"), None),
        P("expert", None),
        P(),
        P(),
    )
    out_specs = (
        P(("patch", "expert"), "hidden"),
        P("expert", None, ("patch", "hidden")),
        P("expert", ("patch", "hidden"), None),
        P("expert", ("patch", "hidden")),
    )
    return jax.shard_map(local, mesh=mesh, in_specs=in_specs, out_specs=out_specs, check_vma=False)
```

```python
import functools

import jax
import jax.numpy as jnp
from jax import lax
from jax.experimental import pallas as pl
from jax.experimental.pallas import tpu as pltpu
from jax.sharding import PartitionSpec as P

inv_root_two = 0.7071067811865476
inv_root_two_pi = 0.3989422804014327


def gelu_parts(pre):
    normal_cdf = 0.5 * (1.0 + lax.erf(pre * inv_root_two))
    density = jnp.exp(-0.5 * pre * pre) * inv_root_two_pi
    return (pre * normal_cdf, normal_cdf + pre * density)


MESH = pl.DeviceIdType.MESH
f32 = jnp.float32
bf16 = jnp.bfloat16
i32 = jnp.int32
PAIR = 16
PIECES = 4
OWN = PIECES // 2
STRIDE = max(1, PIECES // 4)
SUMS = 2
CAP = 128
HALF = CAP // 2
SPILL = 32
FULL = 128


def contract(a, b, dim_a, dim_b):
    return lax.dot_general(a, b, (((dim_a,), (dim_b,)), ((), ())), preferred_element_type=f32)


def marks(mask):
    return jnp.where(mask, 1.0, 0.0).astype(bf16)


def iota(shape, dim):
    return lax.broadcasted_iota(i32, shape, dim)


def split_three(x):
    a = x.astype(bf16)
    rest = x - a.astype(f32)
    b = rest.astype(bf16)
    return (a, b, (rest - b.astype(f32)).astype(bf16))


def row_sums(x):
    ones = jnp.ones((8, x.shape[1]), bf16)
    return sum(contract(ones, part, 1, 1) for part in split_three(x))[0:1]


def previous(x):
    return pltpu.roll(x, 1, 0)


def following(x):
    return pltpu.roll(x, x.shape[0] - 1, 0)


def kernel(
    planes,
    experts,
    tokens,
    cotangent,
    w_in_hbm,
    w_out_hbm,
    gates,
    picks,
    counts,
    window,
    d_tok_hbm,
    d_in_hbm,
    d_out_hbm,
    d_gates,
    misfit,
    codes,
    taken,
    meta,
    tables,
    offs,
    lens,
    pick_sel,
    pack_sel,
    spill_sel,
    held,
    going,
    came,
    spilled,
    allrows,
    win,
    wout,
    act_s,
    back_s,
    home,
    part_out,
    part_in,
    sum_out,
    sum_in,
    grad_go,
    grad_came,
    grad_ret,
    d_tok,
    d_in,
    d_out,
    gate_lo,
    gate_hi,
    gate_all,
    load_sem,
    go_send,
    go_recv,
    spill_send,
    spill_recv,
    ring_send,
    ring_recv,
    twin_send,
    twin_recv,
    part_send,
    part_recv,
    sum_send,
    sum_recv,
    ret_send,
    ret_recv,
    grad_send,
    grad_recv,
    gate_send,
    gate_recv,
    store_sem,
):
    z = lax.axis_index("patch")
    e = lax.axis_index("expert")
    c = lax.axis_index("hidden")
    other = 1 - c
    up = (lax.rem(z + 1, planes), e, c)
    down = (lax.rem(z + planes - 1, planes), e, c)
    twin = (z, e, other)
    piece = held.shape[3]
    pairs = experts * PAIR
    capacity = codes.shape[1]
    plane_peers = [(z, lax.rem(e + k, experts), c) for k in range(1, experts)]
    me = z * 2 + c
    column_ids = [lax.rem(me + k, 2 * planes) for k in range(1, 2 * planes)]
    column_peers = [(i // 2, e, lax.rem(i, 2)) for i in column_ids]

    barrier = pltpu.get_barrier_semaphore()
    for peer in plane_peers + column_peers:
        pl.semaphore_signal(barrier, inc=1, device_id=peer, device_id_type=MESH)

    loads = []
    for a, ref in enumerate((tokens, cotangent)):
        for j in range(OWN):
            col = pl.multiple_of((OWN * c + j) * piece, piece)
            cp = pltpu.make_async_copy(
                ref.at[:, pl.ds(col, piece)], held.at[a, j], load_sem.at[OWN * a + j]
            )
            cp.start()
            loads.append(cp)
    load_in = pltpu.make_async_copy(w_in_hbm, win, load_sem.at[PIECES])
    load_out = pltpu.make_async_copy(w_out_hbm, wout, load_sem.at[PIECES + 1])
    load_in.start()
    load_out.start()

    before = marks(iota((FULL, FULL), 0) < iota((FULL, FULL), 1))
    place = iota((1, capacity), 1)
    for i in range(experts):
        codes[i : i + 1, :] = jnp.where(place < counts[i], picks[i : i + 1, :], -1)
    base = (z * experts + e) * FULL
    wanted = iota((FULL, capacity), 0) + base

    def find(i, carry):
        match = jnp.where(codes[pl.ds(i, 1), :] == wanted, 1.0, 0.0)
        folded = match[:, 0:FULL]
        for k in range(1, capacity // FULL):
            folded += match[:, k * FULL : (k + 1) * FULL]
        taken[pl.ds(i, 1), :] = contract(jnp.ones((8, FULL), bf16), folded.astype(bf16), 1, 1)[0:1]
        return carry

    lax.fori_loop(0, experts, find, 0, unroll=4)
    present = taken[...]
    order = contract(present.astype(bf16), before, 1, 0)
    order = jnp.where(present > 0.5, order, -1.0).astype(i32)
    for i in range(experts):
        pick_sel[i * PAIR : (i + 1) * PAIR, :] = marks(
            iota((PAIR, FULL), 0) == order[i : i + 1, :]
        )

    pl.semaphore_wait(barrier, len(plane_peers) + len(column_peers))

    def remote(src, dst, s, r, dev):
        return pltpu.make_async_remote_copy(
            src_ref=src, dst_ref=dst, send_sem=s, recv_sem=r, device_id=dev, device_id_type=MESH
        )

    own_rows = pl.ds(pl.multiple_of(e * PAIR, PAIR), PAIR)

    def plane_copy(src, dst, ssem, rsem, k):
        to = pl.multiple_of(lax.rem(e + k, experts) * PAIR, PAIR)
        return remote(
            src.at[pl.ds(to, PAIR)], dst.at[own_rows], ssem.at[k], rsem.at[k], plane_peers[k - 1]
        )

    def go_copy(a, j, k):
        return plane_copy(
            going.at[a, j], came.at[a, j], go_send.at[a, j], go_recv.at[a, j], k
        )

    def grad_copy(j, k):
        return plane_copy(
            grad_go.at[j], grad_came.at[j], grad_send.at[j], grad_recv.at[j], k
        )

    def spill_up(a, j):
        return remote(
            spilled.at[a, j, pl.ds(0, SPILL)],
            came.at[a, j, pl.ds(pairs, SPILL)],
            spill_send.at[0, a, j],
            spill_recv.at[0, a, j],
            up,
        )

    def spill_down(a, j):
        return remote(
            spilled.at[a, j, pl.ds(SPILL, SPILL)],
            came.at[a, j, pl.ds(pairs + SPILL, SPILL)],
            spill_send.at[1, a, j],
            spill_recv.at[1, a, j],
            down,
        )

    def ret_down(j):
        return remote(
            grad_go.at[j, pl.ds(pairs, SPILL)],
            grad_ret.at[j, pl.ds(0, SPILL)],
            ret_send.at[0, j],
            ret_recv.at[0, j],
            down,
        )

    def ret_up(j):
        return remote(
            grad_go.at[j, pl.ds(pairs + SPILL, SPILL)],
            grad_ret.at[j, pl.ds(SPILL, SPILL)],
            ret_send.at[1, j],
            ret_recv.at[1, j],
            up,
        )

    def ring_up(a, j, t):
        q = OWN * c + j
        return remote(
            allrows.at[a, q, t, pl.ds(0, HALF)],
            allrows.at[a, q, t + 1, pl.ds(0, HALF)],
            ring_send.at[0, a, j, t],
            ring_recv.at[0, a, j, t + 1],
            up,
        )

    def ring_down(a, j, t):
        q = OWN * c + j
        return remote(
            allrows.at[a, q, t, pl.ds(HALF, HALF)],
            allrows.at[a, q, t + 1, pl.ds(HALF, HALF)],
            ring_send.at[1, a, j, t],
            ring_recv.at[1, a, j, t + 1],
            down,
        )

    def twin_copy(a, j, t):
        q = OWN * c + j
        return remote(
            allrows.at[a, q, t],
            allrows.at[a, q, t],
            twin_send.at[a, j, t],
            twin_recv.at[a, j, t],
            twin,
        )

    def part_copy(j, t):
        slot = lax.rem(t, 2)
        return remote(
            part_out.at[slot, j], part_in.at[t, j], part_send.at[t, j], part_recv.at[t, j], twin
        )

    def sum_up(j, t):
        return remote(
            sum_out.at[lax.rem(t, 2), j, pl.ds(0, HALF)],
            sum_in.at[t, j, pl.ds(0, HALF)],
            sum_send.at[0, j, t],
            sum_recv.at[0, j, t],
            up,
        )

    def sum_down(j, t):
        return remote(
            sum_out.at[lax.rem(t, 2), j, pl.ds(HALF, HALF)],
            sum_in.at[t, j, pl.ds(HALF, HALF)],
            sum_send.at[1, j, t],
            sum_recv.at[1, j, t],
            down,
        )

    for a in range(2):
        for j in range(OWN):
            loads[OWN * a + j].wait()
            going[a, j] = contract(pick_sel[...], held[a, j], 1, 0).astype(bf16)
            came[a, j, own_rows, :] = going[a, j, own_rows, :]
            for k in range(1, experts):
                go_copy(a, j, k).start()

    def forward(p, t):
        a, j = p // OWN, p % OWN

        @pl.when(t < planes)
        def _():
            ring_up(a, j, t - 1).wait_recv()

            @pl.when(t < planes - 1)
            def _():
                ring_up(a, j, t).start()

            ring_down(a, j, t - 1).wait_recv()

            @pl.when(t < planes - 1)
            def _():
                ring_down(a, j, t).start()

            twin_copy(a, j, t).start()

    mine = codes[pl.ds(e, 1), :]
    by_holder = marks((mine >> 7) == iota((FULL, capacity), 0))
    by_row = marks((mine & (FULL - 1)) == iota((FULL, capacity), 0))
    chosen = contract(by_holder, by_row, 1, 1).astype(bf16)
    ranks = contract(chosen, before, 1, 0)
    sizes = contract(chosen, jnp.ones((FULL, FULL), bf16), 1, 0)
    sizes_b = sizes.astype(bf16)
    from_s = iota((FULL, FULL), 1)
    to_s = iota((FULL, FULL), 0)
    ahead = marks((from_s // PAIR == to_s // PAIR) & (from_s < to_s))
    offsets = contract(ahead, sizes_b, 1, 0)
    offs[...] = offsets
    lens[...] = sizes
    group_lane = iota((planes, FULL), 1) // PAIR
    group_row = iota((planes, FULL), 0)
    grouped = marks(group_lane == group_row)
    amount = contract(grouped, sizes_b, 1, 0).astype(i32)
    so_far = contract(marks(group_lane <= group_row), sizes_b, 1, 0).astype(i32)
    live = so_far[planes - 1 : planes, :]
    excess = so_far - ((live * (group_row + 1)) >> 3)
    middle = (jnp.max(excess, axis=0, keepdims=True) + jnp.min(excess, axis=0, keepdims=True)) >> 1
    balanced = window[0] == 0
    begin = jnp.maximum(window[0] - 1, 0) * CAP
    flow = jnp.where(balanced, excess - middle, 0)
    rising = jnp.maximum(flow, 0)
    sinking = jnp.maximum(-flow, 0)
    risen = previous(rising)
    keep = amount - rising - previous(sinking)
    keep = jnp.where(balanced, keep, jnp.clip(amount - begin, 0, CAP))
    up_at = following(keep)
    down_at = previous(keep + risen)
    for i, table in enumerate((keep, rising, risen, sinking)):
        tables[i] = table

    def spread(x):
        return contract(grouped, x.astype(bf16), 0, 0)

    keep_s, rising_s = spread(keep), spread(rising)
    dest = offsets + ranks - begin.astype(f32)
    held_here = balanced | ((dest >= 0) & (dest < keep_s))
    dest -= keep_s
    goes_up = (dest >= 0) & (dest < rising_s)
    goes_down = dest >= rising_s
    spot = jnp.where(
        dest < 0, dest + keep_s, jnp.where(goes_up, spread(up_at) + dest, spread(down_at) + dest - rising_s)
    )
    spot = jnp.where(held_here, spot, -1.0)
    goes_down = (dest >= 0) & goes_down
    shift = jnp.where(goes_up, 1.0, jnp.where(goes_down, -1.0, 0.0))

    def per_slot(x):
        return jnp.sum(
            contract(x.astype(bf16), by_holder, 0, 0) * by_row.astype(f32), axis=0, keepdims=True
        ).astype(i32)

    slot = per_slot(spot)
    block = ((mine >> 11) + per_slot(shift)) & (planes - 1)
    when = jnp.where(slot < HALF, z - block, block - z) & (planes - 1)
    unused = (mine < 0) | (slot < 0)
    meta[0:1, :] = jnp.where(unused, -1, when * CAP + slot)
    meta[1:2, :] = block
    meta[2:3, :] = jnp.where(unused, -1, slot)

    own_group = pl.ds(pl.multiple_of(z * PAIR, PAIR), PAIR)
    widen = marks(iota((PAIR, pairs), 1) // PAIR == iota((PAIR, pairs), 0))
    start = contract(offs[own_group, :].astype(bf16), widen, 0, 0).astype(i32)
    size = contract(lens[own_group, :].astype(bf16), widen, 0, 0).astype(i32)
    index = iota((CAP, pairs), 1) & (PAIR - 1)
    spot_here = jnp.where(index < size, jnp.maximum(start + index - begin, -1), -1)

    def own(i):
        return tables[i, pl.ds(z, 1), :][:, 0:1]

    keep_z, rising_z, risen_z, sinking_z = own(0), own(1), own(2), own(3)
    line = iota((CAP, pairs), 0)
    pack_sel[:, 0:pairs] = marks((spot_here == line) & (line < keep_z))
    lane = iota((CAP, FULL), 1)
    line = iota((CAP, FULL), 0) - keep_z
    pack_sel[:, pairs : pairs + FULL] = marks(
        ((lane < SPILL) & (lane < risen_z) & (line == lane))
        | ((lane >= SPILL) & (lane < SPILL + sinking_z) & (line - risen_z == lane - SPILL))
    )
    line = iota((2 * SPILL, pairs), 0)
    above = spot_here[0 : 2 * SPILL, :] - keep_z
    spill_sel[...] = marks(
        ((line < SPILL) & (line < rising_z) & (above == line))
        | ((line >= SPILL) & (above - rising_z == line - SPILL) & (spot_here[0 : 2 * SPILL, :] >= 0))
    )

    all_codes = codes[...] >> 11
    held_by = [
        jnp.sum(jnp.where(all_codes == i, 1, 0), axis=1, keepdims=True) for i in range(planes)
    ]
    running = [held_by[0]]
    for i in range(1, planes):
        running.append(running[-1] + held_by[i])
    over = [running[i] - ((running[-1] * (i + 1)) >> 3) for i in range(planes)]
    most, least = over[0], over[0]
    for x in over[1:]:
        most, least = jnp.maximum(most, x), jnp.minimum(least, x)
    mid = (most + least) >> 1
    bad = jnp.maximum(most - mid, mid - least) - SPILL
    for i in range(planes):
        leaves = jnp.maximum(over[i] - mid, 0) + jnp.maximum(mid - over[i - 1], 0)
        bad = jnp.maximum(bad, leaves - held_by[i])
    misfit[0] = jnp.max(bad)

    for a in range(2):
        for j in range(OWN):
            came[a, j, pairs + 2 * SPILL :, :] = jnp.zeros((FULL - 2 * SPILL, piece), bf16)
    for a in range(2):
        for j in range(OWN):
            for k in range(1, experts):
                go_copy(a, j, k).wait()
            spilled[a, j] = contract(spill_sel[...], came[a, j, 0:pairs, :], 1, 0).astype(bf16)
            spill_up(a, j).start()
            spill_down(a, j).start()
            for p in range((OWN * a + j) % STRIDE, OWN * a + j, STRIDE):
                forward(p, (OWN * a + j - p) // STRIDE)
            spill_up(a, j).wait()
            spill_down(a, j).wait()
            allrows[a, OWN * c + j, 0] = contract(pack_sel[...], came[a, j], 1, 0).astype(bf16)
            ring_up(a, j, 0).start()
            ring_down(a, j, 0).start()
            twin_copy(a, j, 0).start()
    load_in.wait()
    load_out.wait()

    narrow = home.shape[2]

    def weights(core, j):
        begin = j * narrow
        return win[OWN * core + begin // piece, begin % piece : begin % piece + narrow]

    def step(t, carry):
        for j in range(OWN):
            twin_copy(0, j, t).wait_recv()
        pre = contract(allrows[0, 0, t], win[0], 1, 0)
        for q in range(1, PIECES):
            pre += contract(allrows[0, q, t], win[q], 1, 0)
        act, slope = gelu_parts(pre)
        gate = jnp.sum(
            jnp.where(meta[0:1, :] == iota((CAP, capacity), 0) + t * CAP, gates[...], 0.0),
            axis=1,
            keepdims=True,
        )
        act_s[t] = (gate * act).astype(bf16)

        @pl.when(t > 0)
        def _():
            for p in range(PIECES - STRIDE, PIECES):
                forward(p, t)

        for j in range(OWN):
            twin_copy(1, j, t).wait_recv()
        back = contract(allrows[1, 0, t], wout[:, 0:piece], 1, 1)
        for q in range(1, PIECES):
            back += contract(allrows[1, q, t], wout[:, q * piece : (q + 1) * piece], 1, 1)
        back_pre = (gate * back * slope).astype(bf16)
        back_s[t] = back_pre
        gate_row = row_sums(act * back)
        gate_lo[pl.ds(lax.rem(z + planes - t, planes), 1), :] = gate_row
        gate_hi[pl.ds(lax.rem(z + t, planes), 1), :] = gate_row

        for j in range(SUMS):

            @pl.when(t > 1)
            def _():
                part_copy(j, t - 2).wait_send()

            part_out[lax.rem(t, 2), j] = contract(back_pre, weights(other, j), 1, 1).astype(bf16)
            part_copy(j, t).start()
        for p in range(PIECES - STRIDE):
            forward(p, t + 1 + (PIECES - 1 - p) // STRIDE)
        for j in range(SUMS):
            own_part = contract(back_pre, weights(c, j), 1, 1)
            part_copy(j, t).wait_recv()
            own_part += part_in[t, j].astype(f32)

            @pl.when(t == 0)
            def _():
                home[j] = own_part

            @pl.when(t > 2)
            def _():
                sum_up(j, t - 2).wait_send()
                sum_down(j, t - 2).wait_send()

            @pl.when(t > 1)
            def _():
                sum_up(j, t - 1).wait_recv()
                sum_down(j, t - 1).wait_recv()
                sum_out[lax.rem(t, 2), j] = (own_part + sum_in[t - 1, j].astype(f32)).astype(bf16)

            @pl.when(t == 1)
            def _():
                sum_out[lax.rem(t, 2), j] = own_part.astype(bf16)

            @pl.when(t > 0)
            def _():
                sum_up(j, t).start()
                sum_down(j, t).start()

        return carry

    lax.fori_loop(0, planes, step, 0)

    gate_all[me] = jnp.where(iota(gate_lo.shape, 1) < HALF, gate_lo[...], gate_hi[...])

    def gate_copy(k):
        return remote(
            gate_all.at[me], gate_all.at[me], gate_send.at[k], gate_recv.at[k], column_peers[k - 1]
        )

    for k in range(1, 2 * planes):
        gate_copy(k).start()

    rows = planes * CAP
    act_all = act_s[...].reshape(rows, act_s.shape[2])

    def out_piece(q, carry):
        d_out[q] = contract(act_all, allrows[1, q].reshape(rows, piece), 0, 0).astype(bf16)
        return carry

    lax.fori_loop(0, PIECES, out_piece, 0)

    last = planes - 1
    for j in range(SUMS):
        sum_up(j, last).wait_recv()
        sum_down(j, last).wait_recv()
        slot_grad = (home[j] + sum_in[last, j].astype(f32)).astype(bf16)
        grad_go[j, pairs:, :] = contract(pack_sel[:, pairs:], slot_grad, 0, 0).astype(bf16)
        ret_up(j).start()
        ret_down(j).start()
        grad_go[j, 0:pairs, :] = contract(pack_sel[:, 0:pairs], slot_grad, 0, 0).astype(bf16)
        ret_up(j).wait()
        ret_down(j).wait()
        returned = contract(spill_sel[...], grad_ret[j], 0, 0)
        grad_go[j, 0:pairs, :] = (grad_go[j, 0:pairs, :].astype(f32) + returned).astype(bf16)
        grad_came[j, own_rows, :] = grad_go[j, own_rows, :]
        for k in range(1, experts):
            grad_copy(j, k).start()

    stores = []
    for q in range(PIECES):
        cp = pltpu.make_async_copy(
            d_out.at[q], d_out_hbm.at[:, pl.ds(q * piece, piece)], store_sem.at[q]
        )
        cp.start()
        stores.append(cp)
    back_all = back_s[...].reshape(rows, back_s.shape[2])

    def in_piece(q, carry):
        turned = contract(back_all, allrows[0, q].reshape(rows, piece), 0, 0)
        d_in[q] = turned.T.astype(bf16)
        return carry

    lax.fori_loop(0, PIECES, in_piece, 0)
    for q in range(PIECES):
        cp = pltpu.make_async_copy(d_in.at[q], d_in_hbm.at[q], store_sem.at[PIECES + q])
        cp.start()
        stores.append(cp)

    for k in range(1, 2 * planes):
        gate_copy(k).wait()
    total = gate_all[0]
    for i in range(1, 2 * planes):
        total += gate_all[i]
    own_lanes = pl.ds(pl.multiple_of(z * CAP, CAP), CAP)
    found = marks(meta[2:3, own_lanes] == iota((CAP, CAP), 0))
    values = sum(contract(part, found, 1, 0) for part in split_three(total))
    values = jnp.sum(
        jnp.where(meta[1:2, own_lanes] == iota(values.shape, 0), values, 0.0),
        axis=0,
        keepdims=True,
    )
    d_gates[...] = jnp.where(c == 0, values[:, 0:HALF], values[:, HALF:])

    for j in range(SUMS):
        for k in range(1, experts):
            grad_copy(j, k).wait()
        d_tok[j] = contract(pick_sel[...], grad_came[j], 0, 0).astype(bf16)
        cp = pltpu.make_async_copy(
            d_tok.at[j], d_tok_hbm.at[:, pl.ds(j * narrow, narrow)], store_sem.at[2 * PIECES + j]
        )
        cp.start()
        stores.append(cp)

    for a in range(2):
        for j in range(OWN):
            for t in range(planes):
                twin_copy(a, j, t).wait_send()
                if t < planes - 1:
                    ring_up(a, j, t).wait_send()
                    ring_down(a, j, t).wait_send()
    for j in range(SUMS):
        for t in (planes - 2, planes - 1):
            part_copy(j, t).wait_send()
            sum_up(j, t).wait_send()
            sum_down(j, t).wait_send()
    for cp in stores:
        cp.wait()


def layer(window, tokens, cotangent, w_in, w_out, gates, picks, counts):
    planes = lax.axis_size("patch")
    experts = lax.axis_size("expert")
    tok_dev, width = tokens.shape
    units = w_in.shape[2]
    capacity = picks.shape[1]
    piece = width // PIECES
    narrow = width // 2 // SUMS
    pairs = experts * PAIR
    vmem = pl.BlockSpec(memory_space=pltpu.VMEM)
    smem = pl.BlockSpec(memory_space=pltpu.SMEM)
    hbm = pl.BlockSpec(memory_space=pl.ANY)
    dma = pltpu.SemaphoreType.DMA
    scratch = [
        pltpu.VMEM((experts, capacity), i32),
        pltpu.VMEM((experts, tok_dev), f32),
        pltpu.VMEM((8, capacity), i32),
        pltpu.VMEM((4, planes, FULL), i32),
        pltpu.VMEM((FULL, FULL), f32),
        pltpu.VMEM((FULL, FULL), f32),
        pltpu.VMEM((pairs, tok_dev), bf16),
        pltpu.VMEM((CAP, pairs + FULL), bf16),
        pltpu.VMEM((2 * SPILL, pairs), bf16),
        pltpu.VMEM((2, OWN, tok_dev, piece), bf16),
        pltpu.VMEM((2, OWN, pairs, piece), bf16),
        pltpu.VMEM((2, OWN, pairs + FULL, piece), bf16),
        pltpu.VMEM((2, OWN, 2 * SPILL, piece), bf16),
        pltpu.VMEM((2, PIECES, planes, CAP, piece), bf16),
        pltpu.VMEM((PIECES, piece, units), bf16),
        pltpu.VMEM((units, width), bf16),
        pltpu.VMEM((planes, CAP, units), bf16),
        pltpu.VMEM((planes, CAP, units), bf16),
        pltpu.VMEM((SUMS, CAP, narrow), f32),
        pltpu.VMEM((2, SUMS, CAP, narrow), bf16),
        pltpu.VMEM((planes, SUMS, CAP, narrow), bf16),
        pltpu.VMEM((2, SUMS, CAP, narrow), bf16),
        pltpu.VMEM((planes, SUMS, CAP, narrow), bf16),
        pltpu.VMEM((SUMS, pairs + FULL, narrow), bf16),
        pltpu.VMEM((SUMS, pairs, narrow), bf16),
        pltpu.VMEM((SUMS, 2 * SPILL, narrow), bf16),
        pltpu.VMEM((SUMS, tok_dev, narrow), bf16),
        pltpu.VMEM((PIECES, piece, units), bf16),
        pltpu.VMEM((PIECES, units, piece), bf16),
        pltpu.VMEM((planes, CAP), f32),
        pltpu.VMEM((planes, CAP), f32),
        pltpu.VMEM((2 * planes, planes, CAP), f32),
        dma((PIECES + 2,)),
        dma((2, OWN, experts)),
        dma((2, OWN, experts)),
        dma((2, 2, OWN)),
        dma((2, 2, OWN)),
        dma((2, 2, OWN, planes)),
        dma((2, 2, OWN, planes)),
        dma((2, OWN, planes)),
        dma((2, OWN, planes)),
        dma((planes, SUMS)),
        dma((planes, SUMS)),
        dma((2, SUMS, planes)),
        dma((2, SUMS, planes)),
        dma((2, SUMS)),
        dma((2, SUMS)),
        dma((SUMS, experts)),
        dma((SUMS, experts)),
        dma((2 * planes,)),
        dma((2 * planes,)),
        dma((2 * PIECES + SUMS,)),
    ]
    d_tokens, d_in, d_out, d_gates, misfit = pl.pallas_call(
        functools.partial(kernel, planes, experts),
        out_shape=(
            jax.ShapeDtypeStruct((tok_dev, width // 2), bf16),
            jax.ShapeDtypeStruct((PIECES, piece, units), bf16),
            jax.ShapeDtypeStruct((units, width), bf16),
            jax.ShapeDtypeStruct((1, HALF), f32),
            jax.ShapeDtypeStruct((1,), i32),
        ),
        in_specs=[hbm, hbm, hbm, hbm, vmem, vmem, smem, smem],
        out_specs=(hbm, hbm, hbm, vmem, smem),
        scratch_shapes=scratch,
        compiler_params=pltpu.CompilerParams(
            collective_id=0, has_side_effects=True, vmem_limit_bytes=60 * 2**20
        ),
    )(
        tokens,
        cotangent,
        w_in.reshape(PIECES, piece, units),
        w_out[0],
        gates,
        picks,
        counts,
        jnp.reshape(window, (1,)).astype(i32),
    )
    return (d_tokens, d_in.reshape(w_in.shape), d_out[None], d_gates, misfit)


def store(*refs):
    count = (len(refs) - 2) // 3
    came_sem, went_sem = refs[-2:]
    arriving, leaving = [], []
    for src, dst, mid in zip(refs[:count], refs[count : 2 * count], refs[2 * count :]):
        parts = 4 if src.shape[-2] > FULL else 1
        rows = src.shape[-2] // parts
        for i in range(parts):
            at = pl.ds(i * rows, rows)
            cut = (slice(None), at) if len(src.shape) > 2 else (at,)
            n = len(arriving)
            arriving.append(pltpu.make_async_copy(src.at[cut], mid.at[cut], came_sem.at[n]))
            leaving.append(pltpu.make_async_copy(mid.at[cut], dst.at[cut], went_sem.at[n]))
    for cp in arriving:
        cp.start()
    for first, second in zip(arriving, leaving):
        first.wait()
        second.start()
    for cp in leaving:
        cp.wait()


def local(*args):
    results = layer(0, *args)

    def windows(found, args):
        def add(i, total):
            part = layer(i + 1, *args)[:4]
            return tuple((x.astype(f32) + y.astype(f32)).astype(x.dtype) for x, y in zip(total, part))

        return lax.fori_loop(0, 2, add, tuple(jnp.zeros_like(x) for x in found))

    results = lax.cond(results[4][0] <= 0, lambda found, args: found, windows, results[:4], args)
    hbm = pl.BlockSpec(memory_space=pl.ANY)
    return pl.pallas_call(
        store,
        out_shape=tuple(jax.ShapeDtypeStruct(x.shape, x.dtype) for x in results),
        in_specs=[hbm] * 4,
        out_specs=(hbm,) * 4,
        scratch_shapes=[pltpu.VMEM(x.shape, x.dtype) for x in results]
        + [pltpu.SemaphoreType.DMA((12,))] * 2,
    )(*results)


def solution(mesh):
    in_specs = (
        P(("patch", "expert"), None),
        P(("patch", "expert"), None),
        P("expert", None, ("patch", "hidden")),
        P("expert", ("patch", "hidden"), None),
        P("expert", None),
        P(),
        P(),
    )
    out_specs = (
        P(("patch", "expert"), "hidden"),
        P("expert", None, ("patch", "hidden")),
        P("expert", ("patch", "hidden"), None),
        P("expert", ("patch", "hidden")),
    )
    return jax.shard_map(local, mesh=mesh, in_specs=in_specs, out_specs=out_specs, check_vma=False)
```
